512 devices in a mesh: ex: 32 (over z, core), hid: 16 (over y, x).
Axes of the slice: x: 4, y: 4, z: 16, core: 2. Of those that a mesh axis runs over, the one named last changes fastest.
Arguments:
- tokens: bfloat16 [8192, 2048], P(('ex', 'hid')), may hold values from -6 to 6
- cotangent: bfloat16 [8192, 2048], P(('ex', 'hid')), may hold values from -6 to 6
- gates: float32 [8192, 4], P(('ex', 'hid')), may hold values from 0.1 to 1
- routes: int32 [8192, 4], P(('ex', 'hid')), may hold values from 0 to 63, all different within a row; in each aligned block of 16 rows (0 to 15, 16 to 31, ...) at most 2 rows name the same one
- w_gate: bfloat16 [512, 176, 2048], P(('ex', 'hid')), may hold values from -0.125 to 0.125
- w_up: bfloat16 [512, 176, 2048], P(('ex', 'hid')), may hold values from -0.125 to 0.125
- w_down: bfloat16 [512, 176, 2048], P(('ex', 'hid')), may hold values from -0.15625 to 0.15625
Outputs:
- grad_tokens: bfloat16 [8192, 2048], P(('ex', 'hid'))
The draws below stay inside these ranges and needn't reach their ends.
Inputs may be any that keep to these rules, and one draw needn't show every extreme that they name: `routes`: among the 16 tokens of one device (aligned blocks of rows) no expert is named more than 2 times, a bound that some block reaches; a token's 4 experts differ.
All inputs are finite; a program needn't handle non-finite values.
Results may differ from the reference program's by a relative error of at most 0.007.
Values may be sent and summed in bfloat16 or wider, within the bound.
No kernel may reach another device: no remote copies, remote signals or barrier semaphores. Data moves between devices by JAX's collectives and lax.ppermute only.
A program may use at most 64 MiB of HBM per device.

```python
import math
import jax
import jax.numpy as jnp
import numpy as np
from jax import lax

D = 2048
FF = 1408
TOP = 4
TOK_DEV = 16
EXPERTS = 64
BLOCKS = 8
TOKENS = 8192
SLOT = 2
CAP = 1024
N_EX = 32
N_HID = 16


def level_of(key, extent, cuts, least, high):
    factor_of, own = 1.0, jax.random.fold_in(key, 6)
    for axis_at, parts in cuts:
        steps = jnp.exp(jax.random.uniform(jax.random.fold_in(own, axis_at), (parts,), jnp.float32, least / len(cuts), high / len(cuts)))
        factor_of = factor_of * jnp.repeat(steps, extent[axis_at] // parts).reshape([-1 if axis == axis_at else 1 for axis in range(len(extent))])
    return factor_of


def assign_block(key, own, number, rows, number_of, top, reach, skew):
    ranking = jax.random.permutation(key, number_of)
    heavy_load, usual = portions_of(number_of, rows * top, reach, skew, True), portions_of(number_of, rows * top, reach, skew, False)
    places = jnp.arange(number_of)

    def named(tallies, rotation):
        used = int((tallies > 0).sum())
        fixed = max(1, used // 4)
        moved = fixed + (places - fixed + rotation * (used - fixed)) % max(1, number_of - fixed)
        return jnp.zeros((number_of,), jnp.int32).at[ranking[jnp.where(places < fixed, places, moved)]].set(jnp.asarray(tallies, jnp.int32))

    tallies = jnp.where(number % 4 == 0, named(heavy_load, number // 4), named(usual, number - number // 4 - 1))
    mixed = jax.random.permutation(jax.random.fold_in(own, 3), number_of)
    giver, sink = mixed[0:number_of // 2 * 2:2], mixed[1:number_of // 2 * 2:2]
    margin = jnp.minimum(tallies[giver] - 1, reach - tallies[sink]) // 2
    margin = jnp.where((giver == ranking[0]) | (sink == ranking[0]) | (tallies[sink] == 0), 0, jnp.maximum(margin, 0))
    moved = jax.random.randint(jax.random.fold_in(own, 4), (number_of // 2,), 0, 1 << 20) % (margin + 1)
    tallies = tallies.at[giver].add(-moved).at[sink].add(moved)
    items = jnp.searchsorted(jnp.cumsum(tallies), jnp.arange(rows * top), side="right").astype(jnp.int32)
    table = items.reshape(top, rows).T
    table = table[jax.random.permutation(jax.random.fold_in(own, 1), rows)]
    rotation = jax.random.randint(jax.random.fold_in(own, 2), (rows, 1), 0, top)
    return jnp.take_along_axis(table, (jnp.arange(top)[None, :] + rotation) % top, axis=1)


def portions_of(count, total, most, slope, full):
    weights = [(1 << 20) // math.isqrt(rank ** slope) + 1 for rank in range(1, count + 1)]
    largest = most if full else min(most, max(-(-total // count), total * weights[0] // sum(weights)))
    least = 1 if total - largest >= count - 1 else 0
    given, surplus = [largest] + [least] * (count - 1), total - largest - least * (count - 1)
    while surplus > 0:
        candidates = [i for i in range(1, count) if given[i] < largest] or [i for i in range(1, count) if given[i] < most]
        pool, budget = sum([weights[i] for i in candidates]), surplus
        for i in candidates:
            more = min(most - given[i], max(1, budget * weights[i] // pool), surplus)
            given[i] = given[i] + more
            surplus = surplus - more
    return np.array(given)


def normal_values(own_key, shape, scale, reach, split=(), kind=jnp.bfloat16):
    gain = level_of(own_key, shape, split, -0.22, 0.18) if split else 1.0
    entries = jax.random.normal(own_key, shape, jnp.float32) * scale * gain
    return jnp.minimum(jnp.maximum(entries, -reach), reach).astype(kind)


def setup_inputs(seed: int = 0) -> dict:
    streams_of = jax.random.split(jax.random.key(seed), 8)
    tokens = normal_values(streams_of[0], (TOKENS, D), 1.0, 6.0, ((0, 512),))
    cotangent = normal_values(streams_of[1], (TOKENS, D), 1.0, 6.0, ((0, 512),))
    gates = jnp.clip(jnp.exp(math.log(1.0) - 2.3025851 * jax.random.uniform(streams_of[2], (TOKENS, TOP), jnp.float32) ** level_of(streams_of[2], (TOKENS, TOP), ((0, 512),), -0.2, 0.2)), 0.1, 1.0)
    routes_keys = jax.random.split(jax.random.fold_in(streams_of[3], 1), TOKENS // TOK_DEV)
    routes_turns = jax.random.permutation(jax.random.fold_in(streams_of[3], 3), TOKENS // TOK_DEV)
    routes = jax.vmap(lambda own, number: assign_block(jax.random.fold_in(streams_of[3], 2), own, number, TOK_DEV, EXPERTS, TOP, SLOT, 2))(routes_keys, routes_turns).reshape((TOKENS, TOP))
    w_gate = normal_values(streams_of[4], (EXPERTS * BLOCKS, FF // BLOCKS, D), D ** -0.5, 0.125, ((0, 512),))
    w_up = normal_values(streams_of[5], (EXPERTS * BLOCKS, FF // BLOCKS, D), D ** -0.5, 0.125, ((0, 512),))
    w_down = normal_values(streams_of[6], (EXPERTS * BLOCKS, FF // BLOCKS, D), FF ** -0.5, 0.15625, ((0, 512),))
    return {"tokens": tokens, "cotangent": cotangent, "gates": gates, "routes": routes, "w_gate": w_gate, "w_up": w_up, "w_down": w_down}


def slots_of(flat):
    count = flat.shape[1]
    same = flat[:, :, None] == flat[:, None, :]
    order = jnp.arange(count, dtype=jnp.int32)
    earlier = order[None, :] < order[:, None]
    return lax.optimization_barrier(jnp.sum(jnp.where(same & earlier[None], 1, 0), axis=2)).astype(jnp.int32)

def hidden_grad(inputs, cotan, wgate, wup, wdown):
    dims = (((1,), (1,)), ((), ()))
    gate = lax.dot_general(inputs, wgate, dims, preferred_element_type=jnp.float32)
    upper = lax.dot_general(inputs, wup, dims, preferred_element_type=jnp.float32)
    hidden = lax.dot_general(cotan, wdown, dims, preferred_element_type=jnp.float32)
    sig = jax.nn.sigmoid(gate)
    d_up = (hidden * gate * sig).astype(jnp.bfloat16)
    d_gate = (hidden * upper * sig * (1.0 + gate * (1.0 - sig))).astype(jnp.bfloat16)
    first = jnp.dot(d_gate, wgate, preferred_element_type=jnp.float32)
    second = jnp.dot(d_up, wup, preferred_element_type=jnp.float32)
    return first + second

def reference(tokens, cotangent, gates, routes, w_gate, w_up, w_down):
    devices = N_EX * N_HID
    flat = routes.reshape(devices, TOK_DEV * TOP)
    slot = slots_of(flat)
    device = jnp.arange(devices, dtype=jnp.int32)[:, None]
    source = device // N_HID
    within = device % N_HID
    place = ((within * N_EX + source) * SLOT + slot).reshape(-1).astype(jnp.int32)
    expert_of = routes.reshape(-1)
    assign = jnp.arange(TOKENS * TOP, dtype=jnp.int32)
    x_pad = jnp.concatenate([tokens, jnp.zeros((1, D), jnp.bfloat16)], axis=0)
    dy_pad = jnp.concatenate([cotangent, jnp.zeros((1, D), jnp.bfloat16)], axis=0)
    gate_pad = jnp.concatenate([gates.reshape(-1), jnp.zeros((1,), jnp.float32)])
    width = FF // BLOCKS
    full_gate = w_gate.reshape(EXPERTS, FF, D)
    full_up = w_up.reshape(EXPERTS, FF, D)
    full_down = w_down.reshape(EXPERTS, FF, D)

    def one(acc, inputs):
        wgate, wup, wdown, expert = inputs
        target = jnp.where(expert_of == expert, place, CAP).astype(jnp.int32)
        inverse = jnp.full((CAP,), TOKENS * TOP, jnp.int32).at[target].set(assign, mode='drop')
        owner = inverse // TOP
        rows_x = x_pad[owner]
        rows_dy = (gate_pad[inverse][:, None] * dy_pad[owner].astype(jnp.float32)).astype(jnp.bfloat16)
        total = jnp.zeros((CAP, D), jnp.float32)
        for block in range(BLOCKS):
            lo = block * width
            term = hidden_grad(rows_x, rows_dy, wgate[lo:lo + width, :], wup[lo:lo + width, :], wdown[lo:lo + width, :])
            total = total + lax.optimization_barrier(term.astype(jnp.bfloat16)).astype(jnp.float32)
        result = lax.optimization_barrier(total.astype(jnp.bfloat16)).astype(jnp.float32)
        return (acc.at[owner].add(result), None)
    start = jnp.zeros((TOKENS + 1, D), jnp.float32)
    experts = jnp.arange(EXPERTS, dtype=jnp.int32)
    acc, unused = lax.scan(one, start, (full_gate, full_up, full_down, experts))
    return acc[:TOKENS].astype(jnp.bfloat16)
```

```python
import functools

import jax
import jax.numpy as jnp
from jax import lax
from jax.experimental import pallas as pl
from jax.experimental.pallas import tpu as pltpu
from jax.sharding import PartitionSpec as P

BF = jnp.bfloat16
F32 = jnp.float32
COLS = 4


def _iota(shape, axis):
    return lax.broadcasted_iota(jnp.int32, shape, axis)


def _select(cond):
    return jnp.where(cond, 1.0, 0.0).astype(F32)


def _named(routes, expert):
    tok, top = routes.shape
    each = [_select(routes[:, k : k + 1] == expert) for k in range(top)]
    named = functools.reduce(lambda a, b: a + b, each)
    earlier = _select(_iota((tok, tok), 1) < _iota((tok, tok), 0)).astype(BF)
    slot = jnp.dot(earlier, named.astype(BF), preferred_element_type=F32)
    return each, named, slot


def pack_kernel(tok_ref, cot_ref, gate_ref, route_ref, out_ref):
    g = lax.axis_index("hid") // 8
    tok, width = tok_ref.shape
    top = route_ref.shape[1]
    rows = out_ref.shape[0]
    r = _iota((tok, rows), 1)
    expert = 2 * (r // 8) + jnp.bitwise_xor((r // 4) % 2, g)
    each, named, slot = _named(route_ref[...], expert)
    hit = _select(slot == (r % 2).astype(F32))
    is_x = _select((r // 2) % 2 == 0)
    cot = cot_ref[...].astype(F32)
    parts = [tok_ref[...]]
    picks = [(named * hit * is_x).astype(BF)]
    for k in range(top):
        parts.append((gate_ref[:, k : k + 1] * cot).astype(BF))
        picks.append((each[k] * hit * (1.0 - is_x)).astype(BF))
    data = jnp.concatenate(parts, axis=0)
    pick = jnp.concatenate(picks, axis=0)
    out_ref[...] = lax.dot_general(
        pick, data, (((0,), (0,)), ((), ())), preferred_element_type=F32
    ).astype(BF)


def unpack_kernel(in_ref, own_ref, other_ref):
    rows = own_ref.shape[0]
    half = rows // 2
    q = _iota((rows, in_ref.shape[0]), 0)
    r = _iota((rows, in_ref.shape[0]), 1)
    want = ((q % half) // 2) * 8 + (q // half) * 2 + q % 2
    data = in_ref[...]
    for o, ref in enumerate((own_ref, other_ref)):
        pick = _select(r == want + 4 * o).astype(BF)
        ref[...] = jnp.dot(pick, data, preferred_element_type=F32).astype(BF)


def grad_kernel(*refs):
    n = 4
    rows_in, w_in, outs = refs[:n], refs[n : 2 * n], refs[2 * n : 3 * n]
    x, y, wg, wu, wd, gate, upper, hidden, sem_r, sem_w = refs[3 * n :]
    half = rows_in[0].shape[0] // 2
    unit = w_in[0].shape[0] // 3
    width = x.shape[1]
    step = width // COLS
    row_copies = []
    for i in range(n):
        for m, dst in enumerate((x, y)):
            cp = pltpu.make_async_copy(
                rows_in[i].at[pl.ds(m * half, half)], dst.at[pl.ds(i * half, half)], sem_r.at[2 * i + m]
            )
            cp.start()
            row_copies.append(cp)
    w_copies = []
    for c in range(COLS):
        mine = []
        for m, dst in enumerate((wg, wu, wd)):
            for i in range(n):
                cp = pltpu.make_async_copy(
                    w_in[i].at[pl.ds(m * unit, unit), pl.ds(c * step, step)],
                    dst.at[pl.ds(i * unit, unit), pl.ds(c * step, step)],
                    sem_w.at[(c * 3 + m) * n + i],
                )
                cp.start()
                mine.append(cp)
        w_copies.append(mine)
    for cp in row_copies:
        cp.wait()
    dims = (((1,), (1,)), ((), ()))
    for c in range(COLS):
        for cp in w_copies[c]:
            cp.wait()
        at = slice(c * step, (c + 1) * step)
        for acc, left, right in ((gate, x, wg), (upper, x, wu), (hidden, y, wd)):
            part = lax.dot_general(left[:, at], right[:, at], dims, preferred_element_type=F32)
            if c == 0:
                acc[...] = part
            else:
                acc[...] += part
    gv, uv, hv = gate[...], upper[...], hidden[...]
    sig = jax.nn.sigmoid(gv)
    d_up = (hv * gv * sig).astype(BF)
    d_gate = (hv * uv * sig * (1.0 + gv * (1.0 - sig))).astype(BF)
    for c in range(COLS):
        at = slice(c * step, (c + 1) * step)
        res = jnp.dot(d_gate, wg[:, at], preferred_element_type=F32) + jnp.dot(
            d_up, wu[:, at], preferred_element_type=F32
        )
        for i in range(n):
            outs[i][:, at] = res[i * half : (i + 1) * half].astype(BF)


def merge_kernel(a_ref, b_ref, c_ref, d_ref, out_ref):
    rows = a_ref.shape[0]
    width = out_ref.shape[1]
    own = (a_ref[...].astype(F32) + b_ref[...].astype(F32)).astype(BF)
    other = (c_ref[...].astype(F32) + d_ref[...].astype(F32)).astype(BF)
    data = jnp.concatenate([own[:, :width], own[:, width:], other[:, :width], other[:, width:]], axis=0)
    r = _iota((out_ref.shape[0], 4 * rows), 0)
    q = _iota((out_ref.shape[0], 4 * rows), 1)
    want = ((r // 2) % 2) * 2 * rows + ((r // 4) % 2) * rows + (r // 8) * 2 + r % 2
    out_ref[...] = jnp.dot(
        _select(q == want).astype(BF), data, preferred_element_type=F32
    ).astype(BF)


def final_kernel(in_ref, route_ref, out_ref):
    g = lax.axis_index("hid") // 8
    tok = out_ref.shape[0]
    rows, width = in_ref.shape
    r = _iota((tok, rows), 1)
    expert = 2 * (r // 8) + jnp.bitwise_xor((r // 2) % 2, g)
    _, named, slot = _named(route_ref[...], expert)
    pick = named * _select(slot == (r % 2).astype(F32))
    data = in_ref[...]
    for h in range(2):
        mine = (pick * _select((r // 4) % 2 == h)).astype(BF)
        out_ref[:, h * width : (h + 1) * width] = jnp.dot(
            mine, data, preferred_element_type=F32
        ).astype(BF)


def _shape(*dims):
    return jax.ShapeDtypeStruct(dims, BF)


def _call(kernel, out_shape, name, cost, **kw):
    return pl.pallas_call(
        kernel,
        out_shape=out_shape,
        name=name,
        cost_estimate=pl.CostEstimate(flops=cost[0], bytes_accessed=cost[1], transcendentals=0),
        **kw,
    )


def per_device(tokens, cotangent, gates, routes, w_gate, w_up, w_down):
    n_ex = lax.axis_size("ex")
    n_hid = lax.axis_size("hid")
    side = 4
    tok, width = tokens.shape
    unit = w_gate.shape[1]
    row_of = lambda h, dy, dx: ((h // side) ^ dy) * side + (h % side + dx) % side
    perm = lambda dy, dx: [(h, row_of(h, dy, dx)) for h in range(n_hid)]
    move = lambda v, dy, dx: lax.ppermute(v, "hid", perm(dy, dx))

    weights = jnp.concatenate([w_gate[0], w_up[0], w_down[0]], axis=0)
    w_all = [weights] + [move(weights, 0, d) for d in (1, -1, 2)]

    small = (1 << 26, 1 << 21)
    packed = _call(pack_kernel, _shape(8 * n_ex, width), "pack", small)(tokens, cotangent, gates, routes)
    arrived = lax.all_to_all(packed, "ex", split_axis=0, concat_axis=0, tiled=True)
    own, other = _call(
        unpack_kernel, (_shape(4 * n_ex, width), _shape(4 * n_ex, width)), "unpack", small
    )(arrived)
    rows_all = [own, move(own, 1, 0), move(other, 2, 0), move(other, 3, 0)]

    hid = 4 * unit
    rows = 2 * n_ex
    parts = _call(
        grad_kernel,
        tuple(_shape(rows, width) for _ in range(4)),
        "grad",
        (10 * 4 * rows * hid * width, 6 * hid * width),
        in_specs=[pl.BlockSpec(memory_space=pl.ANY)] * 8,
        scratch_shapes=[
            pltpu.VMEM((4 * rows, width), BF),
            pltpu.VMEM((4 * rows, width), BF),
            pltpu.VMEM((hid, width), BF),
            pltpu.VMEM((hid, width), BF),
            pltpu.VMEM((hid, width), BF),
            pltpu.VMEM((4 * rows, hid), F32),
            pltpu.VMEM((4 * rows, hid), F32),
            pltpu.VMEM((4 * rows, hid), F32),
            pltpu.SemaphoreType.DMA((8,)),
            pltpu.SemaphoreType.DMA((12 * COLS,)),
        ],
        compiler_params=pltpu.CompilerParams(vmem_limit_bytes=40 * 1024 * 1024),
    )(*rows_all, *w_all)
    back = [parts[0]] + [move(parts[d], d, 0) for d in (1, 2, 3)]
    merged = _call(merge_kernel, _shape(8 * n_ex, width // 2), "merge", small)(*back)
    landed = lax.all_to_all(merged, "ex", split_axis=0, concat_axis=0, tiled=True)
    return _call(final_kernel, _shape(tok, width), "final", small)(landed, routes)


def solution(mesh):
    split = P(("ex", "hid"), None)
    deep = P(("ex", "hid"), None, None)
    return jax.shard_map(
        per_device,
        mesh=mesh,
        in_specs=(split, split, split, split, deep, deep, deep),
        out_specs=split,
        check_vma=False,
    )
```

```python
import functools

import jax
import jax.numpy as jnp
from jax import lax
from jax.experimental import pallas as pl
from jax.experimental.pallas import tpu as pltpu
from jax.sharding import PartitionSpec as P

BF = jnp.bfloat16
F32 = jnp.float32
COLS = 4


def _iota(shape, axis):
    return lax.broadcasted_iota(jnp.int32, shape, axis)


def _select(cond):
    return jnp.where(cond, 1.0, 0.0).astype(F32)


def _named(routes, expert):
    tok, top = routes.shape
    each = [_select(routes[:, k : k + 1] == expert) for k in range(top)]
    named = functools.reduce(lambda a, b: a + b, each)
    earlier = _select(_iota((tok, tok), 1) < _iota((tok, tok), 0)).astype(BF)
    slot = jnp.dot(earlier, named.astype(BF), preferred_element_type=F32)
    return each, named, slot


def pack_kernel(tok_ref, cot_ref, gate_ref, route_ref, out_ref):
    tok, width = tok_ref.shape
    top = route_ref.shape[1]
    rows = out_ref.shape[0]
    r = _iota((tok, rows), 1)
    each, named, slot = _named(route_ref[...], r // 4)
    hit = _select(slot == (r % 2).astype(F32))
    is_x = _select((r // 2) % 2 == 0)
    cot = cot_ref[...].astype(F32)
    parts = [tok_ref[...]]
    picks = [(named * hit * is_x).astype(BF)]
    for k in range(top):
        parts.append((gate_ref[:, k : k + 1] * cot).astype(BF))
        picks.append((each[k] * hit * (1.0 - is_x)).astype(BF))
    data = jnp.concatenate(parts, axis=0)
    pick = jnp.concatenate(picks, axis=0)
    out_ref[...] = lax.dot_general(
        pick, data, (((0,), (0,)), ((), ())), preferred_element_type=F32
    ).astype(BF)


def unpack_kernel(in_ref, out_ref):
    rows = out_ref.shape[0] // 4
    half = rows // 2
    q = _iota((rows, in_ref.shape[0]), 0)
    r = _iota((rows, in_ref.shape[0]), 1)
    want = ((q % half) // 2) * 8 + (q // half) * 2 + q % 2
    data = in_ref[...]
    for local in range(2):
        pick = _select(r == want + 4 * local).astype(BF)
        mine = jnp.dot(pick, data, preferred_element_type=F32).astype(BF)
        for y in (2 * local, 2 * local + 1):
            out_ref[y * rows : (y + 1) * rows, :] = mine


def grad_kernel(rows_in, g_in, u_in, d_in, out, x, y, wg, wu, wd, gate, upper, hidden, sem_r, sem_w):
    n = 4
    half = rows_in.shape[0] // (2 * n)
    width = x.shape[1]
    step = width // COLS
    row_copies = []
    for i in range(n):
        for m, dst in enumerate((x, y)):
            cp = pltpu.make_async_copy(
                rows_in.at[pl.ds((2 * i + m) * half, half)], dst.at[pl.ds(i * half, half)], sem_r.at[2 * i + m]
            )
            cp.start()
            row_copies.append(cp)
    w_copies = []
    for c in range(COLS):
        mine = []
        for m, (src, dst) in enumerate(((g_in, wg), (u_in, wu), (d_in, wd))):
            cp = pltpu.make_async_copy(
                src.at[:, pl.ds(c * step, step)], dst.at[:, pl.ds(c * step, step)], sem_w.at[c * 3 + m]
            )
            cp.start()
            mine.append(cp)
        w_copies.append(mine)
    for cp in row_copies:
        cp.wait()
    dims = (((1,), (1,)), ((), ()))
    for c in range(COLS):
        for cp in w_copies[c]:
            cp.wait()
        at = slice(c * step, (c + 1) * step)
        for acc, left, right in ((gate, x, wg), (upper, x, wu), (hidden, y, wd)):
            part = lax.dot_general(left[:, at], right[:, at], dims, preferred_element_type=F32)
            if c == 0:
                acc[...] = part
            else:
                acc[...] += part
    gv, uv, hv = gate[...], upper[...], hidden[...]
    sig = jax.nn.sigmoid(gv)
    d_up = (hv * gv * sig).astype(BF)
    d_gate = (hv * uv * sig * (1.0 + gv * (1.0 - sig))).astype(BF)
    for c in range(COLS):
        at = slice(c * step, (c + 1) * step)
        out[:, at] = (
            jnp.dot(d_gate, wg[:, at], preferred_element_type=F32)
            + jnp.dot(d_up, wu[:, at], preferred_element_type=F32)
        ).astype(BF)


def merge_kernel(in_ref, out_ref):
    rows = in_ref.shape[0] // 4
    width = out_ref.shape[1]
    data = []
    for local in range(2):
        both = [in_ref[y * rows : (y + 1) * rows, :].astype(F32) for y in (2 * local, 2 * local + 1)]
        total = (both[0] + both[1]).astype(BF)
        data += [total[:, :width], total[:, width:]]
    r = _iota((out_ref.shape[0], 4 * rows), 0)
    q = _iota((out_ref.shape[0], 4 * rows), 1)
    want = ((r // 2) % 2) * 2 * rows + ((r // 4) % 2) * rows + (r // 8) * 2 + r % 2
    out_ref[...] = jnp.dot(
        _select(q == want).astype(BF), jnp.concatenate(data, axis=0), preferred_element_type=F32
    ).astype(BF)


def final_kernel(in_ref, route_ref, out_ref):
    tok = out_ref.shape[0]
    rows, width = in_ref.shape
    r = _iota((tok, rows), 1)
    _, named, slot = _named(route_ref[...], 2 * (r // 8) + (r // 2) % 2)
    pick = named * _select(slot == (r % 2).astype(F32))
    data = in_ref[...]
    for h in range(2):
        mine = (pick * _select((r // 4) % 2 == h)).astype(BF)
        out_ref[:, h * width : (h + 1) * width] = jnp.dot(
            mine, data, preferred_element_type=F32
        ).astype(BF)


def _shape(*dims):
    return jax.ShapeDtypeStruct(dims, BF)


def _call(kernel, out_shape, name, cost, **kw):
    return pl.pallas_call(
        kernel,
        out_shape=out_shape,
        name=name,
        cost_estimate=pl.CostEstimate(flops=cost[0], bytes_accessed=cost[1], transcendentals=0),
        **kw,
    )


def per_device(tokens, cotangent, gates, routes, w_gate, w_up, w_down):
    n_ex = lax.axis_size("ex")
    side = 4
    tok, width = tokens.shape
    unit = w_gate.shape[1]
    along_x = [[y * side + x for x in range(side)] for y in range(side)]
    along_y = [[y * side + x for y in range(side)] for x in range(side)]

    gather = lambda w: lax.all_gather(w[0], "hid", axis=0, tiled=True, axis_index_groups=along_x)
    weights = [gather(w) for w in (w_gate, w_up, w_down)]

    def over_y(v):
        return lax.all_to_all(
            v, "hid", split_axis=0, concat_axis=0, tiled=True, axis_index_groups=along_y
        )

    small = (1 << 26, 1 << 21)
    packed = _call(pack_kernel, _shape(8 * n_ex, width), "pack", small)(tokens, cotangent, gates, routes)
    arrived = lax.all_to_all(packed, "ex", split_axis=0, concat_axis=0, tiled=True)
    spread = _call(unpack_kernel, _shape(16 * n_ex, width), "unpack", small)(arrived)
    rows_all = over_y(spread)

    hid = side * unit
    rows = 8 * n_ex
    parts = _call(
        grad_kernel,
        _shape(rows, width),
        "grad",
        (10 * rows * hid * width, 6 * hid * width),
        in_specs=[pl.BlockSpec(memory_space=pltpu.HBM)] * 4,
        scratch_shapes=[
            pltpu.VMEM((rows, width), BF),
            pltpu.VMEM((rows, width), BF),
            pltpu.VMEM((hid, width), BF),
            pltpu.VMEM((hid, width), BF),
            pltpu.VMEM((hid, width), BF),
            pltpu.VMEM((rows, hid), F32),
            pltpu.VMEM((rows, hid), F32),
            pltpu.VMEM((rows, hid), F32),
            pltpu.SemaphoreType.DMA((8,)),
            pltpu.SemaphoreType.DMA((3 * COLS,)),
        ],
        compiler_params=pltpu.CompilerParams(vmem_limit_bytes=40 * 1024 * 1024),
    )(rows_all, *weights)
    merged = _call(merge_kernel, _shape(8 * n_ex, width // 2), "merge", small)(over_y(parts))
    landed = lax.all_to_all(merged, "ex", split_axis=0, concat_axis=0, tiled=True)
    return _call(final_kernel, _shape(tok, width), "final", small)(landed, routes)


def solution(mesh):
    split = P(("ex", "hid"), None)
    deep = P(("ex", "hid"), None, None)
    return jax.shard_map(
        per_device,
        mesh=mesh,
        in_specs=(split, split, split, split, deep, deep, deep),
        out_specs=split,
        check_vma=False,
    )
```

```python
import functools

import jax
import jax.numpy as jnp
from jax import lax
from jax.experimental import pallas as pl
from jax.experimental.pallas import tpu as pltpu
from jax.sharding import PartitionSpec as P

BF = jnp.bfloat16
F32 = jnp.float32
COLS = 4


def _iota(shape, axis):
    return lax.broadcasted_iota(jnp.int32, shape, axis)


def _select(cond):
    return jnp.where(cond, 1.0, 0.0).astype(F32)


def _named(routes, expert):
    top, tok = routes.shape
    each = [_select(routes[k : k + 1, :] == expert) for k in range(top)]
    named = functools.reduce(lambda a, b: a + b, each)
    earlier = _select(_iota((tok, tok), 0) < _iota((tok, tok), 1)).astype(BF)
    slot = jnp.dot(named.astype(BF), earlier, preferred_element_type=F32)
    return each, named, slot


def pack_kernel(tok_ref, cot_ref, gate_ref, route_ref, out_ref):
    tok, width = tok_ref.shape
    top = route_ref.shape[0]
    rows = out_ref.shape[0]
    r = _iota((rows, tok), 0)
    each, named, slot = _named(route_ref[...], r // 4)
    hit = _select(slot == (r % 2).astype(F32))
    is_x = _select((r // 2) % 2 == 0)
    weight = sum(each[k] * gate_ref[k : k + 1, :] for k in range(top))
    weight = jnp.sum(weight * hit * (1.0 - is_x) + is_x * (1.0 / tok), axis=1, keepdims=True)
    pick = named * hit
    pick = jnp.concatenate([pick * is_x, pick * (1.0 - is_x)], axis=1).astype(BF)
    data = jnp.concatenate([tok_ref[...], cot_ref[...]], axis=0)
    out_ref[...] = (weight * jnp.dot(pick, data, preferred_element_type=F32)).astype(BF)


def unpack_kernel(in_ref, out_ref):
    rows = out_ref.shape[0] // 4
    half = rows // 2
    q = _iota((rows, in_ref.shape[0]), 0)
    r = _iota((rows, in_ref.shape[0]), 1)
    want = ((q % half) // 2) * 8 + (q // half) * 2 + q % 2
    data = in_ref[...]
    for local in range(2):
        pick = _select(r == want + 4 * local).astype(BF)
        mine = jnp.dot(pick, data, preferred_element_type=F32).astype(BF)
        for y in (2 * local, 2 * local + 1):
            out_ref[y * rows : (y + 1) * rows, :] = mine


def grad_kernel(rows_in, w_in, out, x, y, wg, wu, wd, gate, upper, hidden, sem_r, sem_w):
    n = 4
    half = rows_in.shape[0] // (2 * n)
    width = x.shape[1]
    step = width // COLS
    row_copies = []
    for i in range(n):
        for m, dst in enumerate((x, y)):
            cp = pltpu.make_async_copy(
                rows_in.at[pl.ds((2 * i + m) * half, half)], dst.at[pl.ds(i * half, half)], sem_r.at[2 * i + m]
            )
            cp.start()
            row_copies.append(cp)
    unit = w_in.shape[0] // (3 * n)
    w_copies = []
    for c in range(COLS):
        mine = []
        for m, dst in enumerate((wg, wu, wd)):
            for i in range(n):
                cp = pltpu.make_async_copy(
                    w_in.at[pl.ds((3 * i + m) * unit, unit), pl.ds(c * step, step)],
                    dst.at[pl.ds(i * unit, unit), pl.ds(c * step, step)],
                    sem_w.at[(c * 3 + m) * n + i],
                )
                cp.start()
                mine.append(cp)
        w_copies.append(mine)
    for cp in row_copies:
        cp.wait()
    dims = (((1,), (1,)), ((), ()))
    for c in range(COLS):
        for cp in w_copies[c]:
            cp.wait()
        at = slice(c * step, (c + 1) * step)
        for acc, left, right in ((gate, x, wg), (upper, x, wu), (hidden, y, wd)):
            part = lax.dot_general(left[:, at], right[:, at], dims, preferred_element_type=F32)
            if c == 0:
                acc[...] = part
            else:
                acc[...] += part
    gv, uv, hv = gate[...], upper[...], hidden[...]
    sig = jax.nn.sigmoid(gv)
    d_up = (hv * gv * sig).astype(BF)
    d_gate = (hv * uv * sig * (1.0 + gv * (1.0 - sig))).astype(BF)
    for c in range(COLS):
        at = slice(c * step, (c + 1) * step)
        out[:, at] = (
            jnp.dot(d_gate, wg[:, at], preferred_element_type=F32)
            + jnp.dot(d_up, wu[:, at], preferred_element_type=F32)
        ).astype(BF)


def merge_kernel(in_ref, out_ref):
    rows = in_ref.shape[0] // 4
    width = out_ref.shape[1]
    data = []
    for local in range(2):
        both = [in_ref[y * rows : (y + 1) * rows, :].astype(F32) for y in (2 * local, 2 * local + 1)]
        total = (both[0] + both[1]).astype(BF)
        data += [total[:, :width], total[:, width:]]
    r = _iota((out_ref.shape[0], 4 * rows), 0)
    q = _iota((out_ref.shape[0], 4 * rows), 1)
    want = ((r // 2) % 2) * 2 * rows + ((r // 4) % 2) * rows + (r // 8) * 2 + r % 2
    out_ref[...] = jnp.dot(
        _select(q == want).astype(BF), jnp.concatenate(data, axis=0), preferred_element_type=F32
    ).astype(BF)


def final_kernel(in_ref, route_ref, out_ref):
    tok = out_ref.shape[0]
    rows, width = in_ref.shape
    r = _iota((rows, tok), 0)
    _, named, slot = _named(route_ref[...], 2 * (r // 8) + (r // 2) % 2)
    pick = named * _select(slot == (r % 2).astype(F32))
    data = in_ref[...]
    for h in range(2):
        mine = (pick * _select((r // 4) % 2 == h)).astype(BF)
        out_ref[:, h * width : (h + 1) * width] = lax.dot_general(
            mine, data, (((0,), (0,)), ((), ())), preferred_element_type=F32
        ).astype(BF)


def _shape(*dims):
    return jax.ShapeDtypeStruct(dims, BF)


def _call(kernel, out_shape, name, cost, vmem=16, **kw):
    return pl.pallas_call(
        kernel,
        out_shape=out_shape,
        name=name,
        cost_estimate=pl.CostEstimate(flops=cost[0], bytes_accessed=cost[1], transcendentals=0),
        compiler_params=pltpu.CompilerParams(vmem_limit_bytes=vmem * 1024 * 1024),
        **kw,
    )


def per_device(tokens, cotangent, gates, routes, w_gate, w_up, w_down):
    n_ex = lax.axis_size("ex")
    side = 4
    tok, width = tokens.shape
    unit = w_gate.shape[1]
    along_x = [[y * side + x for x in range(side)] for y in range(side)]
    along_y = [[y * side + x for y in range(side)] for x in range(side)]

    weights = lax.all_gather(
        jnp.concatenate([w_gate[0], w_up[0], w_down[0]], axis=0),
        "hid",
        axis=0,
        tiled=True,
        axis_index_groups=along_x,
    )

    def over_y(v):
        return lax.all_to_all(
            v, "hid", split_axis=0, concat_axis=0, tiled=True, axis_index_groups=along_y
        )

    small = (1 << 26, 1 << 21)
    packed = _call(pack_kernel, _shape(8 * n_ex, width), "pack", small)(
        tokens, cotangent, gates.T, routes.T
    )
    arrived = lax.all_to_all(packed, "ex", split_axis=0, concat_axis=0, tiled=True)
    spread = _call(unpack_kernel, _shape(16 * n_ex, width), "unpack", small)(arrived)
    rows_all = over_y(spread)

    hid = side * unit
    rows = 8 * n_ex
    parts = _call(
        grad_kernel,
        _shape(rows, width),
        "grad",
        (10 * rows * hid * width, 6 * hid * width),
        in_specs=[pl.BlockSpec(memory_space=pltpu.HBM)] * 2,
        scratch_shapes=[
            pltpu.VMEM((rows, width), BF),
            pltpu.VMEM((rows, width), BF),
            pltpu.VMEM((hid, width), BF),
            pltpu.VMEM((hid, width), BF),
            pltpu.VMEM((hid, width), BF),
            pltpu.VMEM((rows, hid), F32),
            pltpu.VMEM((rows, hid), F32),
            pltpu.VMEM((rows, hid), F32),
            pltpu.SemaphoreType.DMA((8,)),
            pltpu.SemaphoreType.DMA((12 * COLS,)),
        ],
        vmem=56,
    )(rows_all, weights)
    merged = _call(merge_kernel, _shape(8 * n_ex, width // 2), "merge", small)(over_y(parts))
    landed = lax.all_to_all(merged, "ex", split_axis=0, concat_axis=0, tiled=True)
    return _call(final_kernel, _shape(tok, width), "final", small)(landed, routes.T)


def solution(mesh):
    split = P(("ex", "hid"), None)
    deep = P(("ex", "hid"), None, None)
    return jax.shard_map(
        per_device,
        mesh=mesh,
        in_specs=(split, split, split, split, deep, deep, deep),
        out_specs=split,
        check_vma=False,
    )
```

```python
import functools

import jax
import jax.numpy as jnp
from jax import lax
from jax.experimental import pallas as pl
from jax.experimental.pallas import tpu as pltpu
from jax.sharding import PartitionSpec as P

BF = jnp.bfloat16
F32 = jnp.float32
COLS = 4


def _iota(shape, axis):
    return lax.broadcasted_iota(jnp.int32, shape, axis)


def _select(cond):
    return jnp.where(cond, 1.0, 0.0).astype(F32)


def _named(routes, expert):
    top, tok = routes.shape
    each = [_select(routes[k : k + 1, :] == expert) for k in range(top)]
    named = functools.reduce(lambda a, b: a + b, each)
    earlier = _select(_iota((tok, tok), 0) < _iota((tok, tok), 1)).astype(BF)
    slot = jnp.dot(named.astype(BF), earlier, preferred_element_type=F32)
    return each, named, slot


def pack_kernel(tok_ref, cot_ref, gate_ref, route_ref, out_ref):
    tok, width = tok_ref.shape
    top = route_ref.shape[0]
    rows = out_ref.shape[0]
    r = _iota((rows, tok), 0)
    each, named, slot = _named(route_ref[...], r // 4)
    hit = _select(slot == (r % 2).astype(F32))
    is_x = _select((r // 2) % 2 == 0)
    weight = sum(each[k] * gate_ref[k : k + 1, :] for k in range(top))
    weight = jnp.sum(weight * hit * (1.0 - is_x) + is_x * (1.0 / tok), axis=1, keepdims=True)
    pick = named * hit
    pick = jnp.concatenate([pick * is_x, pick * (1.0 - is_x)], axis=1).astype(BF)
    data = jnp.concatenate([tok_ref[...], cot_ref[...]], axis=0)
    out_ref[...] = (weight * jnp.dot(pick, data, preferred_element_type=F32)).astype(BF)


def split_kernel(*refs):
    w_in, outs, sem = refs[:3], refs[3:5], refs[5]
    cut = outs[0].shape[0] // 3
    copies = []
    for m, w in enumerate(w_in):
        for i, (at, size) in enumerate(((0, cut), (cut, w.shape[1] - cut))):
            copies.append(
                pltpu.make_async_copy(
                    w.at[0, pl.ds(at, size)], outs[i].at[pl.ds(m * size, size)], sem.at[2 * m + i]
                )
            )
    for cp in copies:
        cp.start()
    for cp in copies:
        cp.wait()


def unpack_kernel(in_ref, out_ref):
    rows = out_ref.shape[0] // 4
    half = rows // 2
    q = _iota((rows, in_ref.shape[0]), 0)
    r = _iota((rows, in_ref.shape[0]), 1)
    want = ((q % half) // 2) * 8 + (q // half) * 2 + q % 2
    data = in_ref[...]
    for local in range(2):
        pick = _select(r == want + 4 * local).astype(BF)
        mine = jnp.dot(pick, data, preferred_element_type=F32).astype(BF)
        for y in (2 * local, 2 * local + 1):
            out_ref[y * rows : (y + 1) * rows, :] = mine


def grad_kernel(rows_in, *refs):
    n = 4
    own, moved, out = refs[:3], refs[3 : 2 * n + 1], refs[2 * n + 1]
    x, y, wg, wu, wd, gate, upper, hidden, sem_r, sem_w = refs[2 * n + 2 :]
    half = rows_in.shape[0] // (2 * n)
    width = x.shape[1]
    step = width // COLS
    row_copies = []
    for i in range(n):
        for m, dst in enumerate((x, y)):
            cp = pltpu.make_async_copy(
                rows_in.at[pl.ds((2 * i + m) * half, half)], dst.at[pl.ds(i * half, half)], sem_r.at[2 * i + m]
            )
            cp.start()
            row_copies.append(cp)
    unit = own[0].shape[1]
    first = moved[0].shape[0] // 3
    w_copies = []
    for c in range(COLS):
        mine = []
        at = pl.ds(c * step, step)
        for m, dst in enumerate((wg, wu, wd)):
            pieces = [(own[m].at[0, :, at], 0, unit)]
            for i in range(2 * n - 2):
                size = first if i % 2 == 0 else unit - first
                to = unit * (1 + i // 2) + first * (i % 2)
                pieces.append((moved[i].at[pl.ds(m * size, size), at], to, size))
            for i, (src, to, size) in enumerate(pieces):
                cp = pltpu.make_async_copy(
                    src, dst.at[pl.ds(to, size), at], sem_w.at[(c * 3 + m) * (2 * n - 1) + i]
                )
                cp.start()
                mine.append(cp)
        w_copies.append(mine)
    for cp in row_copies:
        cp.wait()
    dims = (((1,), (1,)), ((), ()))
    for c in range(COLS):
        for cp in w_copies[c]:
            cp.wait()
        at = slice(c * step, (c + 1) * step)
        for acc, left, right in ((gate, x, wg), (upper, x, wu), (hidden, y, wd)):
            part = lax.dot_general(left[:, at], right[:, at], dims, preferred_element_type=F32)
            if c == 0:
                acc[...] = part
            else:
                acc[...] += part
    gv, uv, hv = gate[...], upper[...], hidden[...]
    sig = jax.nn.sigmoid(gv)
    d_up = (hv * gv * sig).astype(BF)
    d_gate = (hv * uv * sig * (1.0 + gv * (1.0 - sig))).astype(BF)
    for c in range(COLS):
        at = slice(c * step, (c + 1) * step)
        out[:, at] = (
            jnp.dot(d_gate, wg[:, at], preferred_element_type=F32)
            + jnp.dot(d_up, wu[:, at], preferred_element_type=F32)
        ).astype(BF)


def merge_kernel(in_ref, out_ref):
    rows = in_ref.shape[0] // 4
    width = out_ref.shape[1]
    data = []
    for local in range(2):
        both = [in_ref[y * rows : (y + 1) * rows, :].astype(F32) for y in (2 * local, 2 * local + 1)]
        total = (both[0] + both[1]).astype(BF)
        data += [total[:, :width], total[:, width:]]
    r = _iota((out_ref.shape[0], 4 * rows), 0)
    q = _iota((out_ref.shape[0], 4 * rows), 1)
    want = ((r // 2) % 2) * 2 * rows + ((r // 4) % 2) * rows + (r // 8) * 2 + r % 2
    out_ref[...] = jnp.dot(
        _select(q == want).astype(BF), jnp.concatenate(data, axis=0), preferred_element_type=F32
    ).astype(BF)


def final_kernel(in_ref, route_ref, out_ref):
    tok = out_ref.shape[0]
    rows, width = in_ref.shape
    r = _iota((rows, tok), 0)
    _, named, slot = _named(route_ref[...], 2 * (r // 8) + (r // 2) % 2)
    pick = named * _select(slot == (r % 2).astype(F32))
    data = in_ref[...]
    for h in range(2):
        mine = (pick * _select((r // 4) % 2 == h)).astype(BF)
        out_ref[:, h * width : (h + 1) * width] = lax.dot_general(
            mine, data, (((0,), (0,)), ((), ())), preferred_element_type=F32
        ).astype(BF)


def _shape(*dims):
    return jax.ShapeDtypeStruct(dims, BF)


def _call(kernel, out_shape, name, cost, vmem=16, **kw):
    return pl.pallas_call(
        kernel,
        out_shape=out_shape,
        name=name,
        cost_estimate=pl.CostEstimate(flops=cost[0], bytes_accessed=cost[1], transcendentals=0),
        compiler_params=pltpu.CompilerParams(vmem_limit_bytes=vmem * 1024 * 1024),
        **kw,
    )


def per_device(tokens, cotangent, gates, routes, w_gate, w_up, w_down):
    n_ex = lax.axis_size("ex")
    side = 4
    tok, width = tokens.shape
    unit = w_gate.shape[1]
    along_y = [[y * side + x for y in range(side)] for x in range(side)]

    def shift(v, d):
        return lax.ppermute(
            v, "hid", [(y * side + x, y * side + (x + d) % side) for y in range(side) for x in range(side)]
        )

    cut = (unit // 2 + 15) // 16 * 16
    early, late = _call(
        split_kernel,
        (_shape(3 * cut, width), _shape(3 * (unit - cut), width)),
        "split",
        (0, 12 * unit * width),
        in_specs=[pl.BlockSpec(memory_space=pltpu.HBM)] * 3,
        scratch_shapes=[pltpu.SemaphoreType.DMA((6,))],
    )(w_gate, w_up, w_down)
    def over_y(v):
        return lax.all_to_all(
            v, "hid", split_axis=0, concat_axis=0, tiled=True, axis_index_groups=along_y
        )

    small = (1 << 26, 1 << 21)
    packed = _call(pack_kernel, _shape(8 * n_ex, width), "pack", small)(
        tokens, cotangent, gates.T, routes.T
    )
    arrived = lax.all_to_all(packed, "ex", split_axis=0, concat_axis=0, tiled=True)
    left_early, right_late = shift(early, 1), shift(late, -1)
    left_late, right_early = shift(late, 1), shift(early, -1)
    arrived, left_early, right_late, left_late, right_early = lax.optimization_barrier(
        (arrived, left_early, right_late, left_late, right_early)
    )
    weights = [left_early, left_late, right_early, right_late, shift(left_early, 1), shift(right_late, -1)]
    spread = _call(unpack_kernel, _shape(16 * n_ex, width), "unpack", small)(arrived)
    rows_all = over_y(spread)

    hid = side * unit
    rows = 8 * n_ex
    parts = _call(
        grad_kernel,
        _shape(rows, width),
        "grad",
        (10 * rows * hid * width, 6 * hid * width),
        in_specs=[pl.BlockSpec(memory_space=pl.ANY)] * 10,
        scratch_shapes=[
            pltpu.VMEM((rows, width), BF),
            pltpu.VMEM((rows, width), BF),
            pltpu.VMEM((hid, width), BF),
            pltpu.VMEM((hid, width), BF),
            pltpu.VMEM((hid, width), BF),
            pltpu.VMEM((rows, hid), F32),
            pltpu.VMEM((rows, hid), F32),
            pltpu.VMEM((rows, hid), F32),
            pltpu.SemaphoreType.DMA((8,)),
            pltpu.SemaphoreType.DMA((21 * COLS,)),
        ],
        vmem=56,
    )(rows_all, w_gate, w_up, w_down, *weights)
    merged = _call(merge_kernel, _shape(8 * n_ex, width // 2), "merge", small)(over_y(parts))
    landed = lax.all_to_all(merged, "ex", split_axis=0, concat_axis=0, tiled=True)
    return _call(final_kernel, _shape(tok, width), "final", small)(landed, routes.T)


def solution(mesh):
    split = P(("ex", "hid"), None)
    deep = P(("ex", "hid"), None, None)
    return jax.shard_map(
        per_device,
        mesh=mesh,
        in_specs=(split, split, split, split, deep, deep, deep),
        out_specs=split,
        check_vma=False,
    )
```

```python
import functools

import jax
import jax.numpy as jnp
from jax import lax
from jax.experimental import pallas as pl
from jax.experimental.pallas import tpu as pltpu
from jax.sharding import PartitionSpec as P

BF = jnp.bfloat16
F32 = jnp.float32
COLS = 4


def _iota(shape, axis):
    return lax.broadcasted_iota(jnp.int32, shape, axis)


def _select(cond):
    return jnp.where(cond, 1.0, 0.0).astype(F32)


def _named(routes, expert):
    top, tok = routes.shape
    each = [_select(routes[k : k + 1, :] == expert) for k in range(top)]
    named = functools.reduce(lambda a, b: a + b, each)
    earlier = _select(_iota((tok, tok), 0) < _iota((tok, tok), 1)).astype(BF)
    slot = jnp.dot(named.astype(BF), earlier, preferred_element_type=F32)
    return each, named, slot


def pack_kernel(tok_in, cot_in, gate_in, route_in, out_ref, tok_ref, cot_ref, gate_ref, route_ref, sem):
    copies = [
        pltpu.make_async_copy(src, dst, sem.at[i])
        for i, (src, dst) in enumerate(
            ((route_in, route_ref), (gate_in, gate_ref), (tok_in, tok_ref), (cot_in, cot_ref))
        )
    ]
    for cp in copies:
        cp.start()
    for cp in copies:
        cp.wait()
    tok, width = tok_ref.shape
    top = route_ref.shape[0]
    rows = out_ref.shape[0]
    r = _iota((rows, tok), 0)
    each, named, slot = _named(route_ref[...], r // 4)
    hit = _select(slot == (r % 2).astype(F32))
    is_x = _select((r // 2) % 2 == 0)
    weight = sum(each[k] * gate_ref[k : k + 1, :] for k in range(top))
    weight = jnp.sum(weight * hit * (1.0 - is_x) + is_x * (1.0 / tok), axis=1, keepdims=True)
    pick = named * hit
    pick = jnp.concatenate([pick * is_x, pick * (1.0 - is_x)], axis=1).astype(BF)
    data = jnp.concatenate([tok_ref[...], cot_ref[...]], axis=0)
    out_ref[...] = (weight * jnp.dot(pick, data, preferred_element_type=F32)).astype(BF)


def split_kernel(*refs):
    w_in, outs, sem = refs[:3], refs[3:5], refs[5]
    cut = outs[0].shape[0] // 3
    copies = []
    for m, w in enumerate(w_in):
        for i, (at, size) in enumerate(((0, cut), (cut, w.shape[1] - cut))):
            copies.append(
                pltpu.make_async_copy(
                    w.at[0, pl.ds(at, size)], outs[i].at[pl.ds(m * size, size)], sem.at[2 * m + i]
                )
            )
    for cp in copies:
        cp.start()
    for cp in copies:
        cp.wait()


def unpack_kernel(in_ref, out_ref):
    rows = out_ref.shape[0] // 4
    half = rows // 2
    q = _iota((rows, in_ref.shape[0]), 0)
    r = _iota((rows, in_ref.shape[0]), 1)
    want = ((q % half) // 2) * 8 + (q // half) * 2 + q % 2
    data = in_ref[...]
    for local in range(2):
        pick = _select(r == want + 4 * local).astype(BF)
        mine = jnp.dot(pick, data, preferred_element_type=F32).astype(BF)
        for y in (2 * local, 2 * local + 1):
            out_ref[y * rows : (y + 1) * rows, :] = mine


def grad_kernel(rows_in, *refs):
    n = 4
    own, moved, out = refs[:3], refs[3 : 2 * n + 1], refs[2 * n + 1]
    x, y, wg, wu, wd, sem_r, sem_w = refs[2 * n + 2 :]
    half = rows_in.shape[0] // (2 * n)
    unit, first = own[0].shape[1], moved[0].shape[0] // 3
    each = 2 * n - 1

    def rows_of(m, dst):
        return [
            pltpu.make_async_copy(
                rows_in.at[pl.ds((2 * i + m) * half, half)], dst.at[pl.ds(i * half, half)], sem_r.at[m * n + i]
            )
            for i in range(n)
        ]

    def weight(m, dst):
        pieces = [(own[m].at[0], 0, unit)]
        for i in range(each - 1):
            size = first if i % 2 == 0 else unit - first
            pieces.append((moved[i].at[pl.ds(m * size, size)], unit * (1 + i // 2) + first * (i % 2), size))
        return [
            pltpu.make_async_copy(src, dst.at[pl.ds(to, size)], sem_w.at[m * each + i])
            for i, (src, to, size) in enumerate(pieces)
        ]

    stages = [rows_of(0, x) + weight(0, wg), weight(1, wu), rows_of(1, y) + weight(2, wd)]
    for copies in stages:
        for cp in copies:
            cp.start()
    dims = (((1,), (1,)), ((), ()))
    inner = []
    for copies, left, right in zip(stages, (x, x, y), (wg, wu, wd)):
        for cp in copies:
            cp.wait()
        inner.append(lax.dot_general(left[...], right[...], dims, preferred_element_type=F32))
    gv, uv, hv = inner
    sig = jax.nn.sigmoid(gv)
    d_up = (hv * gv * sig).astype(BF)
    d_gate = (hv * uv * sig * (1.0 + gv * (1.0 - sig))).astype(BF)
    step = x.shape[1] // COLS
    for c in range(COLS):
        at = slice(c * step, (c + 1) * step)
        out[:, at] = (
            jnp.dot(d_gate, wg[:, at], preferred_element_type=F32)
            + jnp.dot(d_up, wu[:, at], preferred_element_type=F32)
        ).astype(BF)


def merge_kernel(in_ref, out_ref):
    rows = in_ref.shape[0] // 4
    width = out_ref.shape[1]
    data = []
    for local in range(2):
        both = [in_ref[y * rows : (y + 1) * rows, :].astype(F32) for y in (2 * local, 2 * local + 1)]
        total = (both[0] + both[1]).astype(BF)
        data += [total[:, :width], total[:, width:]]
    r = _iota((out_ref.shape[0], 4 * rows), 0)
    q = _iota((out_ref.shape[0], 4 * rows), 1)
    want = ((r // 2) % 2) * 2 * rows + ((r // 4) % 2) * rows + (r // 8) * 2 + r % 2
    out_ref[...] = jnp.dot(
        _select(q == want).astype(BF), jnp.concatenate(data, axis=0), preferred_element_type=F32
    ).astype(BF)


def final_kernel(in_ref, route_ref, out_ref):
    tok = out_ref.shape[0]
    rows, width = in_ref.shape
    r = _iota((rows, tok), 0)
    _, named, slot = _named(route_ref[...], 2 * (r // 8) + (r // 2) % 2)
    pick = named * _select(slot == (r % 2).astype(F32))
    data = in_ref[...]
    for h in range(2):
        mine = (pick * _select((r // 4) % 2 == h)).astype(BF)
        out_ref[:, h * width : (h + 1) * width] = lax.dot_general(
            mine, data, (((0,), (0,)), ((), ())), preferred_element_type=F32
        ).astype(BF)


def _shape(*dims):
    return jax.ShapeDtypeStruct(dims, BF)


def _call(kernel, out_shape, name, cost, vmem=16, **kw):
    return pl.pallas_call(
        kernel,
        out_shape=out_shape,
        name=name,
        cost_estimate=pl.CostEstimate(flops=cost[0], bytes_accessed=cost[1], transcendentals=0),
        compiler_params=pltpu.CompilerParams(vmem_limit_bytes=vmem * 1024 * 1024),
        **kw,
    )


def per_device(tokens, cotangent, gates, routes, w_gate, w_up, w_down):
    n_ex = lax.axis_size("ex")
    side = 4
    tok, width = tokens.shape
    unit = w_gate.shape[1]
    along_y = [[y * side + x for y in range(side)] for x in range(side)]

    def shift(v, d):
        return lax.ppermute(
            v, "hid", [(y * side + x, y * side + (x + d) % side) for y in range(side) for x in range(side)]
        )

    cut = (unit // 2 + 15) // 16 * 16
    early, late = _call(
        split_kernel,
        (_shape(3 * cut, width), _shape(3 * (unit - cut), width)),
        "split",
        (0, 12 * unit * width),
        in_specs=[pl.BlockSpec(memory_space=pltpu.HBM)] * 3,
        scratch_shapes=[pltpu.SemaphoreType.DMA((6,))],
    )(w_gate, w_up, w_down)
    def over_y(v):
        return lax.all_to_all(
            v, "hid", split_axis=0, concat_axis=0, tiled=True, axis_index_groups=along_y
        )

    small = (1 << 26, 1 << 21)
    packed = _call(pack_kernel, _shape(8 * n_ex, width), "pack", small, vmem=60,
        in_specs=[pl.BlockSpec(memory_space=pl.ANY)] * 4,
        scratch_shapes=[
            pltpu.VMEM(tokens.shape, BF),
            pltpu.VMEM(tokens.shape, BF),
            pltpu.VMEM(gates.shape[::-1], F32),
            pltpu.VMEM(routes.shape[::-1], jnp.int32),
            pltpu.SemaphoreType.DMA((4,)),
        ],
    )(tokens, cotangent, gates.T, routes.T)
    arrived = lax.all_to_all(packed, "ex", split_axis=0, concat_axis=0, tiled=True)
    left_early, right_late = shift(early, 1), shift(late, -1)
    left_late, right_early = shift(late, 1), shift(early, -1)
    arrived, left_early, right_late, left_late, right_early = lax.optimization_barrier(
        (arrived, left_early, right_late, left_late, right_early)
    )
    weights = [left_early, left_late, right_early, right_late, shift(left_early, 1), shift(right_late, -1)]
    spread = _call(unpack_kernel, _shape(16 * n_ex, width), "unpack", small)(arrived)
    rows_all = over_y(spread)

    hid = side * unit
    rows = 8 * n_ex
    parts = _call(
        grad_kernel,
        _shape(rows, width),
        "grad",
        (10 * rows * hid * width, 6 * hid * width),
        in_specs=[pl.BlockSpec(memory_space=pl.ANY)] * 10,
        scratch_shapes=[
            pltpu.VMEM((rows, width), BF),
            pltpu.VMEM((rows, width), BF),
            pltpu.VMEM((hid, width), BF),
            pltpu.VMEM((hid, width), BF),
            pltpu.VMEM((hid, width), BF),
            pltpu.SemaphoreType.DMA((8,)),
            pltpu.SemaphoreType.DMA((21,)),
        ],
        vmem=60,
    )(rows_all, w_gate, w_up, w_down, *weights)
    merged = _call(merge_kernel, _shape(8 * n_ex, width // 2), "merge", small)(over_y(parts))
    landed = lax.all_to_all(merged, "ex", split_axis=0, concat_axis=0, tiled=True)
    return _call(final_kernel, _shape(tok, width), "final", small)(landed, routes.T)


def solution(mesh):
    split = P(("ex", "hid"), None)
    deep = P(("ex", "hid"), None, None)
    return jax.shard_map(
        per_device,
        mesh=mesh,
        in_specs=(split, split, split, split, deep, deep, deep),
        out_specs=split,
        check_vma=False,
    )
```

```python
import functools

import jax
import jax.numpy as jnp
from jax import lax
from jax.experimental import pallas as pl
from jax.experimental.pallas import tpu as pltpu
from jax.sharding import PartitionSpec as P

BF = jnp.bfloat16
F32 = jnp.float32
COLS = 4


def _iota(shape, axis):
    return lax.broadcasted_iota(jnp.int32, shape, axis)


def _select(cond):
    return jnp.where(cond, 1.0, 0.0).astype(F32)


def _named(routes, expert):
    top, tok = routes.shape
    each = [_select(routes[k : k + 1, :] == expert) for k in range(top)]
    named = functools.reduce(lambda a, b: a + b, each)
    earlier = _select(_iota((tok, tok), 0) < _iota((tok, tok), 1)).astype(BF)
    slot = jnp.dot(named.astype(BF), earlier, preferred_element_type=F32)
    return each, named, slot


def pack_kernel(tok_in, cot_in, gate_in, route_in, out_ref, tok_ref, cot_ref, gate_ref, route_ref, sem):
    copies = [
        pltpu.make_async_copy(src, dst, sem.at[i])
        for i, (src, dst) in enumerate(
            ((route_in, route_ref), (gate_in, gate_ref), (tok_in, tok_ref), (cot_in, cot_ref))
        )
    ]
    for cp in copies:
        cp.start()
    for cp in copies:
        cp.wait()
    tok, width = tok_ref.shape
    top = route_ref.shape[0]
    rows = out_ref.shape[0]
    r = _iota((rows, tok), 0)
    each, named, slot = _named(route_ref[...], r // 4)
    hit = _select(slot == (r % 2).astype(F32))
    is_x = _select((r // 2) % 2 == 0)
    weight = sum(each[k] * gate_ref[k : k + 1, :] for k in range(top))
    weight = jnp.sum(weight * hit * (1.0 - is_x) + is_x * (1.0 / tok), axis=1, keepdims=True)
    pick = named * hit
    pick = jnp.concatenate([pick * is_x, pick * (1.0 - is_x)], axis=1).astype(BF)
    data = jnp.concatenate([tok_ref[...], cot_ref[...]], axis=0)
    out_ref[...] = (weight * jnp.dot(pick, data, preferred_element_type=F32)).astype(BF)


def split_kernel(*refs):
    w_in, outs, sem = refs[:3], refs[3:5], refs[5]
    cut = outs[0].shape[0] // 3
    copies = []
    for m, w in enumerate(w_in):
        for i, (at, size) in enumerate(((0, cut), (cut, w.shape[1] - cut))):
            copies.append(
                pltpu.make_async_copy(
                    w.at[0, pl.ds(at, size)], outs[i].at[pl.ds(m * size, size)], sem.at[2 * m + i]
                )
            )
    for cp in copies:
        cp.start()
    for cp in copies:
        cp.wait()


def unpack_kernel(in_ref, own_ref, other_ref):
    g = lax.axis_index("hid") // 8
    rows = own_ref.shape[0]
    half = rows // 2
    q = _iota((rows, in_ref.shape[0]), 0)
    r = _iota((rows, in_ref.shape[0]), 1)
    want = ((q % half) // 2) * 8 + (q // half) * 2 + q % 2
    data = in_ref[...]
    for o, ref in enumerate((own_ref, other_ref)):
        pick = _select(r == want + 4 * jnp.bitwise_xor(g, o)).astype(BF)
        ref[...] = jnp.dot(pick, data, preferred_element_type=F32).astype(BF)


def _parts(unit, first):
    return [(0, unit)] + [
        (unit * (1 + i // 2) + first * (i % 2), first if i % 2 == 0 else unit - first) for i in range(6)
    ]


def stage_kernel(*refs):
    own, moved, mains, rests, sem = refs[:3], refs[3:7], refs[7:10], refs[10:13], refs[13]
    unit, first = own[0].shape[1], moved[0].shape[0] // 3
    main = mains[0].shape[0]
    copies = []
    for m in range(3):
        for i, (at, size) in enumerate(_parts(unit, first)[:5]):
            src = own[m].at[0] if i == 0 else moved[i - 1].at[pl.ds(m * size, size)]
            fit = min(size, main - at)
            copies.append((src.at[pl.ds(0, fit)], mains[m].at[pl.ds(at, fit)]))
            if fit < size:
                copies.append((src.at[pl.ds(fit, size - fit)], rests[m]))
    copies = [pltpu.make_async_copy(src, dst, sem.at[i]) for i, (src, dst) in enumerate(copies)]
    for cp in copies:
        cp.start()
    for cp in copies:
        cp.wait()


def grad_kernel(*refs):
    n = 4
    rows_in, mains, rests, last, out = refs[:n], refs[n : n + 3], refs[n + 3 : n + 6], refs[n + 6 : n + 8], refs[n + 8]
    x, y, tails = refs[n + 9], refs[n + 10], refs[n + 11 :]
    half = rows_in[0].shape[0] // 2
    me = lax.axis_index("hid") // n
    for i in range(n):
        at = pl.ds(pl.multiple_of(jnp.bitwise_xor(me, i) * half, half), half)
        x[at, :] = rows_in[i][0:half, :]
        y[at, :] = rows_in[i][half : 2 * half, :]
    for m in range(3):
        at = rests[m].shape[0]
        tails[m][0:at, :] = rests[m][...]
        for piece in last:
            size = piece.shape[0] // 3
            tails[m][at : at + size, :] = piece[m * size : (m + 1) * size, :]
            at += size
    dims = (((1,), (1,)), ((), ()))
    dot = lambda a, w: lax.dot_general(a[...], w[...], dims, preferred_element_type=F32)
    inner = []
    for w in (mains, tails):
        gv, uv, hv = dot(x, w[0]), dot(x, w[1]), dot(y, w[2])
        sig = jax.nn.sigmoid(gv)
        d_up = (hv * gv * sig).astype(BF)
        d_gate = (hv * uv * sig * (1.0 + gv * (1.0 - sig))).astype(BF)
        inner.append((d_gate, d_up))
    width = out.shape[1]
    step = width // COLS
    for c in range(COLS):
        at = slice(c * step, (c + 1) * step)
        total = None
        for (d_gate, d_up), w in zip(inner, (mains, tails)):
            for d, ref in ((d_gate, w[0]), (d_up, w[1])):
                part = jnp.dot(d, ref[:, at], preferred_element_type=F32)
                total = part if total is None else total + part
        out[:, at] = total.astype(BF)


def merge_kernel(in_ref, out_ref):
    rows = in_ref.shape[0] // 4
    width = out_ref.shape[1]
    data = []
    for local in range(2):
        both = [in_ref[y * rows : (y + 1) * rows, :].astype(F32) for y in (2 * local, 2 * local + 1)]
        total = (both[0] + both[1]).astype(BF)
        data += [total[:, :width], total[:, width:]]
    r = _iota((out_ref.shape[0], 4 * rows), 0)
    q = _iota((out_ref.shape[0], 4 * rows), 1)
    want = ((r // 2) % 2) * 2 * rows + ((r // 4) % 2) * rows + (r // 8) * 2 + r % 2
    out_ref[...] = jnp.dot(
        _select(q == want).astype(BF), jnp.concatenate(data, axis=0), preferred_element_type=F32
    ).astype(BF)


def final_kernel(in_ref, route_ref, out_ref):
    tok = out_ref.shape[0]
    rows, width = in_ref.shape
    r = _iota((rows, tok), 0)
    _, named, slot = _named(route_ref[...], 2 * (r // 8) + (r // 2) % 2)
    pick = named * _select(slot == (r % 2).astype(F32))
    data = in_ref[...]
    for h in range(2):
        mine = (pick * _select((r // 4) % 2 == h)).astype(BF)
        out_ref[:, h * width : (h + 1) * width] = lax.dot_general(
            mine, data, (((0,), (0,)), ((), ())), preferred_element_type=F32
        ).astype(BF)


def _shape(*dims):
    return jax.ShapeDtypeStruct(dims, BF)


def _call(kernel, out_shape, name, cost, vmem=16, **kw):
    return pl.pallas_call(
        kernel,
        out_shape=out_shape,
        name=name,
        cost_estimate=pl.CostEstimate(flops=cost[0], bytes_accessed=cost[1], transcendentals=0),
        compiler_params=pltpu.CompilerParams(vmem_limit_bytes=vmem * 1024 * 1024),
        **kw,
    )


def per_device(tokens, cotangent, gates, routes, w_gate, w_up, w_down):
    n_ex = lax.axis_size("ex")
    side = 4
    tok, width = tokens.shape
    unit = w_gate.shape[1]
    along_y = [[y * side + x for y in range(side)] for x in range(side)]

    def shift(v, d):
        return lax.ppermute(
            v, "hid", [(y * side + x, y * side + (x + d) % side) for y in range(side) for x in range(side)]
        )

    cut = (unit // 2 + 15) // 16 * 16
    early, late = _call(
        split_kernel,
        (_shape(3 * cut, width), _shape(3 * (unit - cut), width)),
        "split",
        (0, 12 * unit * width),
        in_specs=[pl.BlockSpec(memory_space=pltpu.HBM)] * 3,
        scratch_shapes=[pltpu.SemaphoreType.DMA((6,))],
    )(w_gate, w_up, w_down)
    def over_y(v):
        return lax.all_to_all(
            v, "hid", split_axis=0, concat_axis=0, tiled=True, axis_index_groups=along_y
        )

    small = (1 << 26, 1 << 21)
    packed = _call(pack_kernel, _shape(8 * n_ex, width), "pack", small, vmem=60,
        in_specs=[pl.BlockSpec(memory_space=pl.ANY)] * 4,
        scratch_shapes=[
            pltpu.VMEM(tokens.shape, BF),
            pltpu.VMEM(tokens.shape, BF),
            pltpu.VMEM(gates.shape[::-1], F32),
            pltpu.VMEM(routes.shape[::-1], jnp.int32),
            pltpu.SemaphoreType.DMA((4,)),
        ],
    )(tokens, cotangent, gates.T, routes.T)
    arrived = lax.all_to_all(packed, "ex", split_axis=0, concat_axis=0, tiled=True)
    left_early, right_late = shift(early, 1), shift(late, -1)
    left_late, right_early = shift(late, 1), shift(early, -1)
    arrived, left_early, right_late, left_late, right_early = lax.optimization_barrier(
        (arrived, left_early, right_late, left_late, right_early)
    )
    last = [shift(left_early, 1), shift(right_late, -1)]
    own, other = _call(unpack_kernel, (_shape(4 * n_ex, width),) * 2, "unpack", small)(arrived)
    flip = lambda v, d: lax.ppermute(
        v, "hid", [(y * side + x, (y ^ d) * side + x) for y in range(side) for x in range(side)]
    )
    rows_all = [own, flip(own, 1), flip(other, 2), flip(other, 3)]
    hid = side * unit
    main = 3 * unit // 256 * 256
    rest = 3 * unit - main
    _, *pieces = lax.optimization_barrier((own, left_early, left_late, right_early, right_late))
    staged = _call(
        stage_kernel,
        (_shape(main, width),) * 3 + (_shape(rest, width),) * 3,
        "stage",
        (0, 24 * 3 * unit * width),
        in_specs=[pl.BlockSpec(memory_space=pl.ANY)] * 7,
        scratch_shapes=[pltpu.SemaphoreType.DMA((18,))],
    )(w_gate, w_up, w_down, *pieces)
    rows = 8 * n_ex
    parts = _call(
        grad_kernel,
        _shape(rows, width),
        "grad",
        (10 * rows * hid * width, 6 * hid * width),
        vmem=36,
        scratch_shapes=[pltpu.VMEM((rows, width), BF)] * 2 + [pltpu.VMEM((rest + unit, width), BF)] * 3,
    )(*rows_all, *staged, *last)
    merged = _call(merge_kernel, _shape(8 * n_ex, width // 2), "merge", small)(over_y(parts))
    landed = lax.all_to_all(merged, "ex", split_axis=0, concat_axis=0, tiled=True)
    return _call(final_kernel, _shape(tok, width), "final", small)(landed, routes.T)


def solution(mesh):
    split = P(("ex", "hid"), None)
    deep = P(("ex", "hid"), None, None)
    return jax.shard_map(
        per_device,
        mesh=mesh,
        in_specs=(split, split, split, split, deep, deep, deep),
        out_specs=split,
        check_vma=False,
    )
```

```python
import functools

import jax
import jax.numpy as jnp
from jax import lax
from jax.experimental import pallas as pl
from jax.experimental.pallas import tpu as pltpu
from jax.sharding import PartitionSpec as P

BF = jnp.bfloat16
F32 = jnp.float32
COLS = 4


def _iota(shape, axis):
    return lax.broadcasted_iota(jnp.int32, shape, axis)


def _select(cond):
    return jnp.where(cond, 1.0, 0.0).astype(F32)


def _named(routes, expert):
    top, tok = routes.shape
    each = [_select(routes[k : k + 1, :] == expert) for k in range(top)]
    named = functools.reduce(lambda a, b: a + b, each)
    earlier = _select(_iota((tok, tok), 0) < _iota((tok, tok), 1)).astype(BF)
    slot = jnp.dot(named.astype(BF), earlier, preferred_element_type=F32)
    return each, named, slot


def pack_kernel(tok_in, cot_in, gate_in, route_in, out_ref, tok_ref, cot_ref, gate_ref, route_ref, sem):
    copies = [
        pltpu.make_async_copy(src, dst, sem.at[i])
        for i, (src, dst) in enumerate(
            ((route_in, route_ref), (gate_in, gate_ref), (tok_in, tok_ref), (cot_in, cot_ref))
        )
    ]
    for cp in copies:
        cp.start()
    for cp in copies[:2]:
        cp.wait()
    tok, width = tok_ref.shape
    top = route_ref.shape[0]
    rows = out_ref.shape[0]
    r = _iota((rows, tok), 0)
    each, named, slot = _named(route_ref[...], r // 4)
    hit = _select(slot == (r % 2).astype(F32))
    is_x = _select((r // 2) % 2 == 0)
    weight = sum(each[k] * gate_ref[k : k + 1, :] for k in range(top))
    weight = jnp.sum(weight * hit * (1.0 - is_x) + is_x * (1.0 / tok), axis=1, keepdims=True)
    pick = named * hit
    pick = jnp.concatenate([pick * is_x, pick * (1.0 - is_x)], axis=1).astype(BF)
    for cp in copies[2:]:
        cp.wait()
    data = jnp.concatenate([tok_ref[...], cot_ref[...]], axis=0)
    out_ref[...] = (weight * jnp.dot(pick, data, preferred_element_type=F32)).astype(BF)


def split_kernel(*refs):
    w_in, outs, sem = refs[:3], refs[3:5], refs[5]
    cut = outs[0].shape[0] // 3
    copies = []
    for m, w in enumerate(w_in):
        for i, (at, size) in enumerate(((0, cut), (cut, w.shape[1] - cut))):
            copies.append(
                pltpu.make_async_copy(
                    w.at[0, pl.ds(at, size)], outs[i].at[pl.ds(m * size, size)], sem.at[2 * m + i]
                )
            )
    for cp in copies:
        cp.start()
    for cp in copies:
        cp.wait()


def unpack_kernel(in_ref, own_ref, other_ref):
    g = lax.axis_index("hid") // 8
    rows = own_ref.shape[0]
    half = rows // 2
    q = _iota((rows, in_ref.shape[0]), 0)
    r = _iota((rows, in_ref.shape[0]), 1)
    want = ((q % half) // 2) * 8 + (q // half) * 2 + q % 2
    data = in_ref[...]
    for o, ref in enumerate((own_ref, other_ref)):
        pick = _select(r == want + 4 * jnp.bitwise_xor(g, o)).astype(BF)
        ref[...] = jnp.dot(pick, data, preferred_element_type=F32).astype(BF)


def _parts(unit, first):
    return [(0, unit)] + [
        (unit * (1 + i // 2) + first * (i % 2), first if i % 2 == 0 else unit - first) for i in range(6)
    ]


def stage_kernel(*refs):
    own, moved, mains, rests, sem = refs[:3], refs[3:7], refs[7:10], refs[10:13], refs[13]
    unit, first = own[0].shape[1], moved[0].shape[0] // 3
    main = mains[0].shape[0]
    copies = []
    for m in range(3):
        for i, (at, size) in enumerate(_parts(unit, first)[:5]):
            src = own[m].at[0] if i == 0 else moved[i - 1].at[pl.ds(m * size, size)]
            fit = min(size, main - at)
            copies.append((src.at[pl.ds(0, fit)], mains[m].at[pl.ds(at, fit)]))
            if fit < size:
                copies.append((src.at[pl.ds(fit, size - fit)], rests[m]))
    copies = [pltpu.make_async_copy(src, dst, sem.at[i]) for i, (src, dst) in enumerate(copies)]
    for cp in copies:
        cp.start()
    for cp in copies:
        cp.wait()


def grad_kernel(*refs):
    n = 4
    rows_in, mains, rests, last, out = refs[:n], refs[n : n + 3], refs[n + 3 : n + 6], refs[n + 6 : n + 8], refs[n + 8]
    x, y, tails = refs[n + 9], refs[n + 10], refs[n + 11 :]
    half = rows_in[0].shape[0] // 2
    me = lax.axis_index("hid") // n
    for i in range(n):
        at = pl.ds(pl.multiple_of(jnp.bitwise_xor(me, i) * half, half), half)
        x[at, :] = rows_in[i][0:half, :]
        y[at, :] = rows_in[i][half : 2 * half, :]
    for m in range(3):
        at = rests[m].shape[0]
        tails[m][0:at, :] = rests[m][...]
        for piece in last:
            size = piece.shape[0] // 3
            tails[m][at : at + size, :] = piece[m * size : (m + 1) * size, :]
            at += size
    dims = (((1,), (1,)), ((), ()))
    dot = lambda a, w: lax.dot_general(a[...], w[...], dims, preferred_element_type=F32)
    inner = []
    for w in (mains, tails):
        gv, uv, hv = dot(x, w[0]), dot(x, w[1]), dot(y, w[2])
        sig = jax.nn.sigmoid(gv)
        d_up = (hv * gv * sig).astype(BF)
        d_gate = (hv * uv * sig * (1.0 + gv * (1.0 - sig))).astype(BF)
        inner.append((d_gate, d_up))
    width = out.shape[1]
    step = width // COLS
    for c in range(COLS):
        at = slice(c * step, (c + 1) * step)
        total = None
        for (d_gate, d_up), w in zip(inner, (mains, tails)):
            for d, ref in ((d_gate, w[0]), (d_up, w[1])):
                part = jnp.dot(d, ref[:, at], preferred_element_type=F32)
                total = part if total is None else total + part
        out[:, at] = total.astype(BF)


def merge_kernel(in_ref, out_ref):
    rows = in_ref.shape[0] // 4
    width = out_ref.shape[1]
    data = []
    for local in range(2):
        both = [in_ref[y * rows : (y + 1) * rows, :].astype(F32) for y in (2 * local, 2 * local + 1)]
        total = (both[0] + both[1]).astype(BF)
        data += [total[:, :width], total[:, width:]]
    r = _iota((out_ref.shape[0], 4 * rows), 0)
    q = _iota((out_ref.shape[0], 4 * rows), 1)
    want = ((r // 2) % 2) * 2 * rows + ((r // 4) % 2) * rows + (r // 8) * 2 + r % 2
    out_ref[...] = jnp.dot(
        _select(q == want).astype(BF), jnp.concatenate(data, axis=0), preferred_element_type=F32
    ).astype(BF)


def final_kernel(in_ref, route_ref, out_ref):
    tok = out_ref.shape[0]
    rows, width = in_ref.shape
    r = _iota((rows, tok), 0)
    _, named, slot = _named(route_ref[...], 2 * (r // 8) + (r // 2) % 2)
    pick = named * _select(slot == (r % 2).astype(F32))
    data = in_ref[...]
    for h in range(2):
        mine = (pick * _select((r // 4) % 2 == h)).astype(BF)
        out_ref[:, h * width : (h + 1) * width] = lax.dot_general(
            mine, data, (((0,), (0,)), ((), ())), preferred_element_type=F32
        ).astype(BF)


def _shape(*dims):
    return jax.ShapeDtypeStruct(dims, BF)


def _call(kernel, out_shape, name, cost, vmem=16, **kw):
    return pl.pallas_call(
        kernel,
        out_shape=out_shape,
        name=name,
        cost_estimate=pl.CostEstimate(flops=cost[0], bytes_accessed=cost[1], transcendentals=0),
        compiler_params=pltpu.CompilerParams(vmem_limit_bytes=vmem * 1024 * 1024),
        **kw,
    )


def per_device(tokens, cotangent, gates, routes, w_gate, w_up, w_down):
    n_ex = lax.axis_size("ex")
    side = 4
    tok, width = tokens.shape
    unit = w_gate.shape[1]
    along_y = [[y * side + x for y in range(side)] for x in range(side)]

    def shift(v, d):
        return lax.ppermute(
            v, "hid", [(y * side + x, y * side + (x + d) % side) for y in range(side) for x in range(side)]
        )

    cut = (unit // 2 + 15) // 16 * 16
    early, late = _call(
        split_kernel,
        (_shape(3 * cut, width), _shape(3 * (unit - cut), width)),
        "split",
        (0, 12 * unit * width),
        in_specs=[pl.BlockSpec(memory_space=pltpu.HBM)] * 3,
        scratch_shapes=[pltpu.SemaphoreType.DMA((6,))],
    )(w_gate, w_up, w_down)
    def over_y(v):
        return lax.all_to_all(
            v, "hid", split_axis=0, concat_axis=0, tiled=True, axis_index_groups=along_y
        )

    small = (1 << 26, 1 << 21)
    packed = _call(pack_kernel, _shape(8 * n_ex, width), "pack", small, vmem=60,
        in_specs=[pl.BlockSpec(memory_space=pl.ANY)] * 4,
        scratch_shapes=[
            pltpu.VMEM(tokens.shape, BF),
            pltpu.VMEM(tokens.shape, BF),
            pltpu.VMEM(gates.shape[::-1], F32),
            pltpu.VMEM(routes.shape[::-1], jnp.int32),
            pltpu.SemaphoreType.DMA((4,)),
        ],
    )(tokens, cotangent, gates.T, routes.T)
    arrived = lax.all_to_all(packed, "ex", split_axis=0, concat_axis=0, tiled=True)
    left_early, right_late = shift(early, 1), shift(late, -1)
    left_late, right_early = shift(late, 1), shift(early, -1)
    own, other = _call(unpack_kernel, (_shape(4 * n_ex, width),) * 2, "unpack", small)(arrived)
    own, other, left_early, right_late, left_late, right_early = lax.optimization_barrier(
        (own, other, left_early, right_late, left_late, right_early)
    )
    last = [shift(left_early, 1), shift(right_late, -1)]
    flip = lambda v, d: lax.ppermute(
        v, "hid", [(y * side + x, (y ^ d) * side + x) for y in range(side) for x in range(side)]
    )
    two, three = flip(other, 2), flip(other, 3)
    rows_all = [own, flip(own, 1), two, three]
    hid = side * unit
    main = 3 * unit // 256 * 256
    rest = 3 * unit - main
    staged = _call(
        stage_kernel,
        (_shape(main, width),) * 3 + (_shape(rest, width),) * 3,
        "stage",
        (0, 24 * 3 * unit * width),
        in_specs=[pl.BlockSpec(memory_space=pl.ANY)] * 7,
        scratch_shapes=[pltpu.SemaphoreType.DMA((18,))],
    )(w_gate, w_up, w_down, left_early, left_late, right_early, right_late)
    rows = 8 * n_ex
    parts = _call(
        grad_kernel,
        _shape(rows, width),
        "grad",
        (10 * rows * hid * width, 6 * hid * width),
        vmem=36,
        scratch_shapes=[pltpu.VMEM((rows, width), BF)] * 2 + [pltpu.VMEM((rest + unit, width), BF)] * 3,
    )(*rows_all, *staged, *last)
    merged = _call(merge_kernel, _shape(8 * n_ex, width // 2), "merge", small)(over_y(parts))
    landed = lax.all_to_all(merged, "ex", split_axis=0, concat_axis=0, tiled=True)
    return _call(final_kernel, _shape(tok, width), "final", small)(landed, routes.T)


def solution(mesh):
    split = P(("ex", "hid"), None)
    deep = P(("ex", "hid"), None, None)
    return jax.shard_map(
        per_device,
        mesh=mesh,
        in_specs=(split, split, split, split, deep, deep, deep),
        out_specs=split,
        check_vma=False,
    )
```

```python
import functools

import jax
import jax.numpy as jnp
from jax import lax
from jax.experimental import pallas as pl
from jax.experimental.pallas import tpu as pltpu
from jax.sharding import PartitionSpec as P

BF = jnp.bfloat16
F32 = jnp.float32
COLS = 4


def _iota(shape, axis):
    return lax.broadcasted_iota(jnp.int32, shape, axis)


def _select(cond):
    return jnp.where(cond, 1.0, 0.0).astype(F32)


def _named(routes, expert):
    top, tok = routes.shape
    each = [_select(routes[k : k + 1, :] == expert) for k in range(top)]
    named = functools.reduce(lambda a, b: a + b, each)
    earlier = _select(_iota((tok, tok), 0) < _iota((tok, tok), 1)).astype(BF)
    slot = jnp.dot(named.astype(BF), earlier, preferred_element_type=F32)
    return each, named, slot


def pack_kernel(tok_in, cot_in, gate_in, route_in, out_ref, tok_ref, cot_ref, gate_ref, route_ref, sem):
    copies = [
        pltpu.make_async_copy(src, dst, sem.at[i])
        for i, (src, dst) in enumerate(
            ((route_in, route_ref), (gate_in, gate_ref), (tok_in, tok_ref), (cot_in, cot_ref))
        )
    ]
    for cp in copies:
        cp.start()
    for cp in copies[:2]:
        cp.wait()
    tok, width = tok_ref.shape
    top = route_ref.shape[0]
    rows = out_ref.shape[0]
    r = _iota((rows, tok), 0)
    each, named, slot = _named(route_ref[...], r // 4)
    hit = _select(slot == (r % 2).astype(F32))
    is_x = _select((r // 2) % 2 == 0)
    weight = sum(each[k] * gate_ref[k : k + 1, :] for k in range(top))
    weight = jnp.sum(weight * hit * (1.0 - is_x) + is_x * (1.0 / tok), axis=1, keepdims=True)
    pick = named * hit
    pick = jnp.concatenate([pick * is_x, pick * (1.0 - is_x)], axis=1).astype(BF)
    for cp in copies[2:]:
        cp.wait()
    data = jnp.concatenate([tok_ref[...], cot_ref[...]], axis=0)
    out_ref[...] = (weight * jnp.dot(pick, data, preferred_element_type=F32)).astype(BF)


def split_kernel(*refs):
    w_in, outs, sem = refs[:3], refs[3:5], refs[5]
    cut = outs[0].shape[0] // 3
    copies = []
    for m, w in enumerate(w_in):
        for i, (at, size) in enumerate(((0, cut), (cut, w.shape[1] - cut))):
            copies.append(
                pltpu.make_async_copy(
                    w.at[0, pl.ds(at, size)], outs[i].at[pl.ds(m * size, size)], sem.at[2 * m + i]
                )
            )
    for cp in copies:
        cp.start()
    for cp in copies:
        cp.wait()


def unpack_kernel(in_ref, own_ref, other_ref):
    g = lax.axis_index("hid") // 8
    rows = own_ref.shape[0]
    half = rows // 2
    q = _iota((rows, in_ref.shape[0]), 0)
    r = _iota((rows, in_ref.shape[0]), 1)
    want = ((q % half) // 2) * 8 + (q // half) * 2 + q % 2
    data = in_ref[...]
    for o, ref in enumerate((own_ref, other_ref)):
        pick = _select(r == want + 4 * jnp.bitwise_xor(g, o)).astype(BF)
        ref[...] = jnp.dot(pick, data, preferred_element_type=F32).astype(BF)


def _parts(unit, first):
    return [(0, unit)] + [
        (unit * (1 + i // 2) + first * (i % 2), first if i % 2 == 0 else unit - first) for i in range(6)
    ]


def stage_kernel(*refs):
    own, moved, mains, rests, sem = refs[:3], refs[3:7], refs[7:10], refs[10:13], refs[13]
    unit, first = own[0].shape[1], moved[0].shape[0] // 3
    main = mains[0].shape[0]
    copies = []
    for m in range(3):
        for i, (at, size) in enumerate(_parts(unit, first)[:5]):
            src = own[m].at[0] if i == 0 else moved[i - 1].at[pl.ds(m * size, size)]
            fit = min(size, main - at)
            copies.append((src.at[pl.ds(0, fit)], mains[m].at[pl.ds(at, fit)]))
            if fit < size:
                copies.append((src.at[pl.ds(fit, size - fit)], rests[m]))
    copies = [pltpu.make_async_copy(src, dst, sem.at[i]) for i, (src, dst) in enumerate(copies)]
    for cp in copies:
        cp.start()
    for cp in copies:
        cp.wait()


def grad_kernel(*refs):
    n = 4
    rows_in, mains, rests, last, out = refs[:n], refs[n : n + 3], refs[n + 3 : n + 6], refs[n + 6 : n + 8], refs[n + 8]
    x, y, tails = refs[n + 9], refs[n + 10], refs[n + 11 :]
    half = rows_in[0].shape[0] // 2
    me = lax.axis_index("hid") // n
    for i, d in enumerate((2, 3, 1, 0)):
        at = pl.ds(pl.multiple_of(jnp.bitwise_xor(me, d) * half, half), half)
        x[at, :] = rows_in[i][0:half, :]
        y[at, :] = rows_in[i][half : 2 * half, :]
    for m in range(3):
        at = rests[m].shape[0]
        tails[m][0:at, :] = rests[m][...]
        for piece in last:
            size = piece.shape[0] // 3
            tails[m][at : at + size, :] = piece[m * size : (m + 1) * size, :]
            at += size
    dims = (((1,), (1,)), ((), ()))
    dot = lambda a, w: lax.dot_general(a[...], w[...], dims, preferred_element_type=F32)
    inner = []
    for w in (mains, tails):
        gv, uv, hv = dot(x, w[0]), dot(x, w[1]), dot(y, w[2])
        sig = jax.nn.sigmoid(gv)
        d_up = (hv * gv * sig).astype(BF)
        d_gate = (hv * uv * sig * (1.0 + gv * (1.0 - sig))).astype(BF)
        inner.append((d_gate, d_up))
    width = out.shape[1]
    step = width // COLS
    for c in range(COLS):
        at = slice(c * step, (c + 1) * step)
        total = None
        for (d_gate, d_up), w in zip(inner, (mains, tails)):
            for d, ref in ((d_gate, w[0]), (d_up, w[1])):
                part = jnp.dot(d, ref[:, at], preferred_element_type=F32)
                total = part if total is None else total + part
        out[:, at] = total.astype(BF)


def merge_kernel(in_ref, out_ref):
    rows = in_ref.shape[0] // 4
    width = out_ref.shape[1]
    data = []
    for local in range(2):
        both = [in_ref[y * rows : (y + 1) * rows, :].astype(F32) for y in (2 * local, 2 * local + 1)]
        total = (both[0] + both[1]).astype(BF)
        data += [total[:, :width], total[:, width:]]
    r = _iota((out_ref.shape[0], 4 * rows), 0)
    q = _iota((out_ref.shape[0], 4 * rows), 1)
    want = ((r // 2) % 2) * 2 * rows + ((r // 4) % 2) * rows + (r // 8) * 2 + r % 2
    out_ref[...] = jnp.dot(
        _select(q == want).astype(BF), jnp.concatenate(data, axis=0), preferred_element_type=F32
    ).astype(BF)


def final_kernel(in_ref, route_ref, out_ref):
    tok = out_ref.shape[0]
    rows, width = in_ref.shape
    r = _iota((rows, tok), 0)
    _, named, slot = _named(route_ref[...], 2 * (r // 8) + (r // 2) % 2)
    pick = named * _select(slot == (r % 2).astype(F32))
    data = in_ref[...]
    for h in range(2):
        mine = (pick * _select((r // 4) % 2 == h)).astype(BF)
        out_ref[:, h * width : (h + 1) * width] = lax.dot_general(
            mine, data, (((0,), (0,)), ((), ())), preferred_element_type=F32
        ).astype(BF)


def _shape(*dims):
    return jax.ShapeDtypeStruct(dims, BF)


def _call(kernel, out_shape, name, cost, vmem=16, **kw):
    return pl.pallas_call(
        kernel,
        out_shape=out_shape,
        name=name,
        cost_estimate=pl.CostEstimate(flops=cost[0], bytes_accessed=cost[1], transcendentals=0),
        compiler_params=pltpu.CompilerParams(vmem_limit_bytes=vmem * 1024 * 1024),
        **kw,
    )


def per_device(tokens, cotangent, gates, routes, w_gate, w_up, w_down):
    n_ex = lax.axis_size("ex")
    side = 4
    tok, width = tokens.shape
    unit = w_gate.shape[1]
    along_y = [[y * side + x for y in range(side)] for x in range(side)]

    def shift(v, d):
        return lax.ppermute(
            v, "hid", [(y * side + x, y * side + (x + d) % side) for y in range(side) for x in range(side)]
        )

    cut = (unit // 2 + 15) // 16 * 16
    early, late = _call(
        split_kernel,
        (_shape(3 * cut, width), _shape(3 * (unit - cut), width)),
        "split",
        (0, 12 * unit * width),
        in_specs=[pl.BlockSpec(memory_space=pltpu.HBM)] * 3,
        scratch_shapes=[pltpu.SemaphoreType.DMA((6,))],
    )(w_gate, w_up, w_down)
    def over_y(v):
        return lax.all_to_all(
            v, "hid", split_axis=0, concat_axis=0, tiled=True, axis_index_groups=along_y
        )

    small = (1 << 26, 1 << 21)
    packed = _call(pack_kernel, _shape(8 * n_ex, width), "pack", small, vmem=60,
        in_specs=[pl.BlockSpec(memory_space=pl.ANY)] * 4,
        scratch_shapes=[
            pltpu.VMEM(tokens.shape, BF),
            pltpu.VMEM(tokens.shape, BF),
            pltpu.VMEM(gates.shape[::-1], F32),
            pltpu.VMEM(routes.shape[::-1], jnp.int32),
            pltpu.SemaphoreType.DMA((4,)),
        ],
    )(tokens, cotangent, gates.T, routes.T)
    arrived = lax.all_to_all(packed, "ex", split_axis=0, concat_axis=0, tiled=True)
    left_early, right_late = shift(early, 1), shift(late, -1)
    left_late, right_early = shift(late, 1), shift(early, -1)
    own, other = _call(unpack_kernel, (_shape(4 * n_ex, width),) * 2, "unpack", small)(arrived)
    own, left_early, right_late = lax.optimization_barrier((own, left_early, right_late))
    last = [shift(left_early, 1), shift(right_late, -1)]
    own, other, left_late, right_early = lax.optimization_barrier((own, other, left_late, right_early))
    flip = lambda v, d: lax.ppermute(
        v, "hid", [(y * side + x, (y ^ d) * side + x) for y in range(side) for x in range(side)]
    )
    rows_all = [flip(other, 2), flip(other, 3), flip(own, 1), own]
    hid = side * unit
    main = 3 * unit // 256 * 256
    rest = 3 * unit - main
    staged = _call(
        stage_kernel,
        (_shape(main, width),) * 3 + (_shape(rest, width),) * 3,
        "stage",
        (0, 24 * 3 * unit * width),
        in_specs=[pl.BlockSpec(memory_space=pl.ANY)] * 7,
        scratch_shapes=[pltpu.SemaphoreType.DMA((18,))],
    )(w_gate, w_up, w_down, left_early, left_late, right_early, right_late)
    rows = 8 * n_ex
    parts = _call(
        grad_kernel,
        _shape(rows, width),
        "grad",
        (10 * rows * hid * width, 6 * hid * width),
        vmem=36,
        scratch_shapes=[pltpu.VMEM((rows, width), BF)] * 2 + [pltpu.VMEM((rest + unit, width), BF)] * 3,
    )(*rows_all, *staged, *last)
    merged = _call(merge_kernel, _shape(8 * n_ex, width // 2), "merge", small)(over_y(parts))
    landed = lax.all_to_all(merged, "ex", split_axis=0, concat_axis=0, tiled=True)
    return _call(final_kernel, _shape(tok, width), "final", small)(landed, routes.T)


def solution(mesh):
    split = P(("ex", "hid"), None)
    deep = P(("ex", "hid"), None, None)
    return jax.shard_map(
        per_device,
        mesh=mesh,
        in_specs=(split, split, split, split, deep, deep, deep),
        out_specs=split,
        check_vma=False,
    )
```

```python
import functools

import jax
import jax.numpy as jnp
from jax import lax
from jax.experimental import pallas as pl
from jax.experimental.pallas import tpu as pltpu
from jax.sharding import PartitionSpec as P

BF = jnp.bfloat16
F32 = jnp.float32
COLS = 4


def _iota(shape, axis):
    return lax.broadcasted_iota(jnp.int32, shape, axis)


def _select(cond):
    return jnp.where(cond, 1.0, 0.0).astype(F32)


def _named(routes, expert):
    top, tok = routes.shape
    each = [_select(routes[k : k + 1, :] == expert) for k in range(top)]
    named = functools.reduce(lambda a, b: a + b, each)
    earlier = _select(_iota((tok, tok), 0) < _iota((tok, tok), 1)).astype(BF)
    slot = jnp.dot(named.astype(BF), earlier, preferred_element_type=F32)
    return each, named, slot


def pack_kernel(tok_in, cot_in, gate_in, route_in, out_ref, tok_ref, cot_ref, gate_ref, route_ref, sem):
    copies = [
        pltpu.make_async_copy(src, dst, sem.at[i])
        for i, (src, dst) in enumerate(
            ((route_in, route_ref), (gate_in, gate_ref), (tok_in, tok_ref), (cot_in, cot_ref))
        )
    ]
    for cp in copies:
        cp.start()
    for cp in copies[:2]:
        cp.wait()
    tok, width = tok_ref.shape
    top = route_ref.shape[0]
    rows = out_ref.shape[0]
    r = _iota((rows, tok), 0)
    each, named, slot = _named(route_ref[...], r // 4)
    hit = _select(slot == (r % 2).astype(F32))
    is_x = _select((r // 2) % 2 == 0)
    weight = sum(each[k] * gate_ref[k : k + 1, :] for k in range(top))
    weight = jnp.sum(weight * hit * (1.0 - is_x) + is_x * (1.0 / tok), axis=1, keepdims=True)
    pick = named * hit
    pick = jnp.concatenate([pick * is_x, pick * (1.0 - is_x)], axis=1).astype(BF)
    for cp in copies[2:]:
        cp.wait()
    data = jnp.concatenate([tok_ref[...], cot_ref[...]], axis=0)
    out_ref[...] = (weight * jnp.dot(pick, data, preferred_element_type=F32)).astype(BF)


def split_kernel(*refs):
    w_in, outs, sem = refs[:3], refs[3:5], refs[5]
    cut = outs[0].shape[0] // 3
    copies = []
    for m, w in enumerate(w_in):
        for i, (at, size) in enumerate(((0, cut), (cut, w.shape[1] - cut))):
            copies.append(
                pltpu.make_async_copy(
                    w.at[0, pl.ds(at, size)], outs[i].at[pl.ds(m * size, size)], sem.at[2 * m + i]
                )
            )
    for cp in copies:
        cp.start()
    for cp in copies:
        cp.wait()


def unpack_kernel(in_ref, own_ref, other_ref):
    g = lax.axis_index("hid") // 8
    rows = own_ref.shape[0]
    half = rows // 2
    q = _iota((rows, in_ref.shape[0]), 0)
    r = _iota((rows, in_ref.shape[0]), 1)
    want = ((q % half) // 2) * 8 + (q // half) * 2 + q % 2
    data = in_ref[...]
    for o, ref in enumerate((own_ref, other_ref)):
        pick = _select(r == want + 4 * jnp.bitwise_xor(g, o)).astype(BF)
        ref[...] = jnp.dot(pick, data, preferred_element_type=F32).astype(BF)


def _parts(unit, first):
    return [(0, unit)] + [
        (unit * (1 + i // 2) + first * (i % 2), first if i % 2 == 0 else unit - first) for i in range(6)
    ]


def stage_kernel(*refs):
    own, moved, mains, rests, sem = refs[:3], refs[3:7], refs[7:10], refs[10:13], refs[13]
    unit, first = own[0].shape[1], moved[0].shape[0] // 3
    main = mains[0].shape[0]
    copies = []
    for m in range(3):
        for i, (at, size) in enumerate(_parts(unit, first)[:5]):
            src = own[m].at[0] if i == 0 else moved[i - 1].at[pl.ds(m * size, size)]
            fit = min(size, main - at)
            copies.append((src.at[pl.ds(0, fit)], mains[m].at[pl.ds(at, fit)]))
            if fit < size:
                copies.append((src.at[pl.ds(fit, size - fit)], rests[m]))
    copies = [pltpu.make_async_copy(src, dst, sem.at[i]) for i, (src, dst) in enumerate(copies)]
    for cp in copies:
        cp.start()
    for cp in copies:
        cp.wait()


def grad_kernel(*refs):
    n = 4
    rows_in, mains, rests, last, out = refs[:n], refs[n : n + 3], refs[n + 3 : n + 6], refs[n + 6 : n + 8], refs[n + 8]
    x, y, tails = refs[n + 9], refs[n + 10], refs[n + 11 :]
    half = rows_in[0].shape[0] // 2
    me = lax.axis_index("hid") // n
    for i, d in enumerate((2, 3, 1, 0)):
        at = pl.ds(pl.multiple_of(jnp.bitwise_xor(me, d) * half, half), half)
        x[at, :] = rows_in[i][0:half, :]
        y[at, :] = rows_in[i][half : 2 * half, :]
    for m in range(3):
        at = rests[m].shape[0]
        tails[m][0:at, :] = rests[m][...]
        for piece in last:
            size = piece.shape[0] // 3
            tails[m][at : at + size, :] = piece[m * size : (m + 1) * size, :]
            at += size
    dims = (((1,), (1,)), ((), ()))
    dot = lambda a, w: lax.dot_general(a[...], w[...], dims, preferred_element_type=F32)
    inner = []
    for w in (mains, tails):
        gv, uv, hv = dot(x, w[0]), dot(x, w[1]), dot(y, w[2])
        sig = jax.nn.sigmoid(gv)
        d_up = (hv * gv * sig).astype(BF)
        d_gate = (hv * uv * sig * (1.0 + gv * (1.0 - sig))).astype(BF)
        inner.append((d_gate, d_up))
    width = out.shape[1]
    step = width // COLS
    for c in range(COLS):
        at = slice(c * step, (c + 1) * step)
        total = None
        for (d_gate, d_up), w in zip(inner, (mains, tails)):
            for d, ref in ((d_gate, w[0]), (d_up, w[1])):
                part = jnp.dot(d, ref[:, at], preferred_element_type=F32)
                total = part if total is None else total + part
        out[:, at] = total.astype(BF)


def merge_kernel(in_ref, out_ref):
    rows = in_ref.shape[0] // 4
    width = out_ref.shape[1]
    data = []
    for local in range(2):
        both = [in_ref[y * rows : (y + 1) * rows, :].astype(F32) for y in (2 * local, 2 * local + 1)]
        total = (both[0] + both[1]).astype(BF)
        data += [total[:, :width], total[:, width:]]
    r = _iota((out_ref.shape[0], 4 * rows), 0)
    q = _iota((out_ref.shape[0], 4 * rows), 1)
    want = ((r // 2) % 2) * 2 * rows + ((r // 4) % 2) * rows + (r // 8) * 2 + r % 2
    out_ref[...] = jnp.dot(
        _select(q == want).astype(BF), jnp.concatenate(data, axis=0), preferred_element_type=F32
    ).astype(BF)


def final_kernel(in_ref, route_ref, out_ref):
    tok = out_ref.shape[0]
    rows, width = in_ref.shape
    r = _iota((rows, tok), 0)
    _, named, slot = _named(route_ref[...], 2 * (r // 8) + (r // 2) % 2)
    pick = named * _select(slot == (r % 2).astype(F32))
    data = in_ref[...]
    for h in range(2):
        mine = (pick * _select((r // 4) % 2 == h)).astype(BF)
        out_ref[:, h * width : (h + 1) * width] = lax.dot_general(
            mine, data, (((0,), (0,)), ((), ())), preferred_element_type=F32
        ).astype(BF)


def _shape(*dims):
    return jax.ShapeDtypeStruct(dims, BF)


def _call(kernel, out_shape, name, cost, vmem=16, **kw):
    return pl.pallas_call(
        kernel,
        out_shape=out_shape,
        name=name,
        cost_estimate=pl.CostEstimate(flops=cost[0], bytes_accessed=cost[1], transcendentals=0),
        compiler_params=pltpu.CompilerParams(vmem_limit_bytes=vmem * 1024 * 1024),
        **kw,
    )


def per_device(tokens, cotangent, gates, routes, w_gate, w_up, w_down):
    n_ex = lax.axis_size("ex")
    side = 4
    tok, width = tokens.shape
    unit = w_gate.shape[1]
    along_y = [[y * side + x for y in range(side)] for x in range(side)]

    def shift(v, d):
        return lax.ppermute(
            v, "hid", [(y * side + x, y * side + (x + d) % side) for y in range(side) for x in range(side)]
        )

    cut = (unit // 2 + 15) // 16 * 16
    early, late = _call(
        split_kernel,
        (_shape(3 * cut, width), _shape(3 * (unit - cut), width)),
        "split",
        (0, 12 * unit * width),
        in_specs=[pl.BlockSpec(memory_space=pltpu.HBM)] * 3,
        scratch_shapes=[pltpu.SemaphoreType.DMA((6,))],
    )(w_gate, w_up, w_down)
    def over_y(v):
        return lax.all_to_all(
            v, "hid", split_axis=0, concat_axis=0, tiled=True, axis_index_groups=along_y
        )

    small = (1 << 26, 1 << 21)
    packed = _call(pack_kernel, _shape(8 * n_ex, width), "pack", small, vmem=60,
        in_specs=[pl.BlockSpec(memory_space=pl.ANY)] * 4,
        scratch_shapes=[
            pltpu.VMEM(tokens.shape, BF),
            pltpu.VMEM(tokens.shape, BF),
            pltpu.VMEM(gates.shape[::-1], F32),
            pltpu.VMEM(routes.shape[::-1], jnp.int32),
            pltpu.SemaphoreType.DMA((4,)),
        ],
    )(tokens, cotangent, gates.T, routes.T)
    arrived = lax.all_to_all(packed, "ex", split_axis=0, concat_axis=0, tiled=True)
    left_early, right_late = shift(early, 1), shift(late, -1)
    left_late, right_early = shift(late, 1), shift(early, -1)
    own, other = _call(unpack_kernel, (_shape(4 * n_ex, width),) * 2, "unpack", small)(arrived)
    last = [shift(left_early, 1), shift(right_late, -1)]
    flip = lambda v, d: lax.ppermute(
        v, "hid", [(y * side + x, (y ^ d) * side + x) for y in range(side) for x in range(side)]
    )
    rows_all = [flip(other, 2), flip(other, 3), flip(own, 1), own]
    hid = side * unit
    main = 3 * unit // 256 * 256
    rest = 3 * unit - main
    staged = _call(
        stage_kernel,
        (_shape(main, width),) * 3 + (_shape(rest, width),) * 3,
        "stage",
        (0, 24 * 3 * unit * width),
        in_specs=[pl.BlockSpec(memory_space=pl.ANY)] * 7,
        scratch_shapes=[pltpu.SemaphoreType.DMA((18,))],
    )(w_gate, w_up, w_down, left_early, left_late, right_early, right_late)
    rows = 8 * n_ex
    parts = _call(
        grad_kernel,
        _shape(rows, width),
        "grad",
        (10 * rows * hid * width, 6 * hid * width),
        vmem=36,
        scratch_shapes=[pltpu.VMEM((rows, width), BF)] * 2 + [pltpu.VMEM((rest + unit, width), BF)] * 3,
    )(*rows_all, *staged, *last)
    merged = _call(merge_kernel, _shape(8 * n_ex, width // 2), "merge", small)(over_y(parts))
    landed = lax.all_to_all(merged, "ex", split_axis=0, concat_axis=0, tiled=True)
    return _call(final_kernel, _shape(tok, width), "final", small)(landed, routes.T)


def solution(mesh):
    split = P(("ex", "hid"), None)
    deep = P(("ex", "hid"), None, None)
    return jax.shard_map(
        per_device,
        mesh=mesh,
        in_specs=(split, split, split, split, deep, deep, deep),
        out_specs=split,
        check_vma=False,
    )
```

```python
import functools

import jax
import jax.numpy as jnp
from jax import lax
from jax.experimental import pallas as pl
from jax.experimental.pallas import tpu as pltpu
from jax.sharding import PartitionSpec as P

BF = jnp.bfloat16
F32 = jnp.float32
COLS = 4


def _iota(shape, axis):
    return lax.broadcasted_iota(jnp.int32, shape, axis)


def _select(cond):
    return jnp.where(cond, 1.0, 0.0).astype(F32)


def _named(routes, expert):
    top, tok = routes.shape
    each = [_select(routes[k : k + 1, :] == expert) for k in range(top)]
    named = functools.reduce(lambda a, b: a + b, each)
    earlier = _select(_iota((tok, tok), 0) < _iota((tok, tok), 1)).astype(BF)
    slot = jnp.dot(named.astype(BF), earlier, preferred_element_type=F32)
    return each, named, slot


def pack_kernel(tok_in, cot_in, gate_in, route_in, out_ref, tok_ref, cot_ref, gate_ref, route_ref, sem):
    copies = [
        pltpu.make_async_copy(src, dst, sem.at[i])
        for i, (src, dst) in enumerate(
            ((route_in, route_ref), (gate_in, gate_ref), (tok_in, tok_ref), (cot_in, cot_ref))
        )
    ]
    for cp in copies:
        cp.start()
    for cp in copies[:2]:
        cp.wait()
    tok, width = tok_ref.shape
    top = route_ref.shape[0]
    rows = out_ref.shape[0]
    r = _iota((rows, tok), 0)
    each, named, slot = _named(route_ref[...], r // 4)
    hit = _select(slot == (r % 2).astype(F32))
    is_x = _select((r // 2) % 2 == 0)
    weight = sum(each[k] * gate_ref[k : k + 1, :] for k in range(top))
    weight = jnp.sum(weight * hit * (1.0 - is_x) + is_x * (1.0 / tok), axis=1, keepdims=True)
    pick = named * hit
    pick = jnp.concatenate([pick * is_x, pick * (1.0 - is_x)], axis=1).astype(BF)
    for cp in copies[2:]:
        cp.wait()
    data = jnp.concatenate([tok_ref[...], cot_ref[...]], axis=0)
    out_ref[...] = (weight * jnp.dot(pick, data, preferred_element_type=F32)).astype(BF)


def split_kernel(*refs):
    w_in, outs, sem = refs[:3], refs[3:5], refs[5]
    cut = outs[0].shape[0] // 3
    copies = []
    for m, w in enumerate(w_in):
        for i, (at, size) in enumerate(((0, cut), (cut, w.shape[1] - cut))):
            copies.append(
                pltpu.make_async_copy(
                    w.at[0, pl.ds(at, size)], outs[i].at[pl.ds(m * size, size)], sem.at[2 * m + i]
                )
            )
    for cp in copies:
        cp.start()
    for cp in copies:
        cp.wait()


def unpack_kernel(in_ref, own_ref, other_ref):
    g = lax.axis_index("hid") // 8
    rows = own_ref.shape[0]
    half = rows // 2
    q = _iota((rows, in_ref.shape[0]), 0)
    r = _iota((rows, in_ref.shape[0]), 1)
    want = ((q % half) // 2) * 8 + (q // half) * 2 + q % 2
    data = in_ref[...]
    for o, ref in enumerate((own_ref, other_ref)):
        pick = _select(r == want + 4 * jnp.bitwise_xor(g, o)).astype(BF)
        ref[...] = jnp.dot(pick, data, preferred_element_type=F32).astype(BF)


def _parts(unit, first):
    return [(0, unit)] + [
        (unit * (1 + i // 2) + first * (i % 2), first if i % 2 == 0 else unit - first) for i in range(6)
    ]


def stage_kernel(*refs):
    own, moved, mains, rests, sem = refs[:3], refs[3:7], refs[7:10], refs[10:13], refs[13]
    unit, first = own[0].shape[1], moved[0].shape[0] // 3
    main = mains[0].shape[0]
    copies = []
    for m in range(3):
        for i, (at, size) in enumerate(_parts(unit, first)[:5]):
            src = own[m].at[0] if i == 0 else moved[i - 1].at[pl.ds(m * size, size)]
            fit = min(size, main - at)
            copies.append((src.at[pl.ds(0, fit)], mains[m].at[pl.ds(at, fit)]))
            if fit < size:
                copies.append((src.at[pl.ds(fit, size - fit)], rests[m]))
    copies = [pltpu.make_async_copy(src, dst, sem.at[i]) for i, (src, dst) in enumerate(copies)]
    for cp in copies:
        cp.start()
    for cp in copies:
        cp.wait()


def grad_kernel(*refs):
    n = 4
    rows_in, mains, rests, last, out = refs[:n], refs[n : n + 3], refs[n + 3 : n + 6], refs[n + 6 : n + 8], refs[n + 8]
    x, y, tails, sem = refs[n + 9], refs[n + 10], refs[n + 11 : n + 14], refs[n + 14]
    copies = []
    for m in range(3):
        at = rests[m].shape[0]
        for piece in last:
            size = piece.shape[0] // 3
            copies.append(
                pltpu.make_async_copy(
                    piece.at[pl.ds(m * size, size)], tails[m].at[pl.ds(at, size)], sem.at[len(copies)]
                )
            )
            at += size
    for cp in copies:
        cp.start()
    half = rows_in[0].shape[0] // 2
    me = lax.axis_index("hid") // n
    for i, d in enumerate((2, 3, 1, 0)):
        at = pl.ds(pl.multiple_of(jnp.bitwise_xor(me, d) * half, half), half)
        x[at, :] = rows_in[i][0:half, :]
        y[at, :] = rows_in[i][half : 2 * half, :]
    dims = (((1,), (1,)), ((), ()))
    dot = lambda a, w: lax.dot_general(a[...], w[...], dims, preferred_element_type=F32)
    inner = []
    for w in (mains, tails):
        if w is tails:
            for m in range(3):
                tails[m][0 : rests[m].shape[0], :] = rests[m][...]
            for cp in copies:
                cp.wait()
        gv, uv, hv = dot(x, w[0]), dot(x, w[1]), dot(y, w[2])
        sig = jax.nn.sigmoid(gv)
        d_up = (hv * gv * sig).astype(BF)
        d_gate = (hv * uv * sig * (1.0 + gv * (1.0 - sig))).astype(BF)
        inner.append((d_gate, d_up))
    width = out.shape[1]
    step = width // COLS
    for c in range(COLS):
        at = slice(c * step, (c + 1) * step)
        total = None
        for (d_gate, d_up), w in zip(inner, (mains, tails)):
            for d, ref in ((d_gate, w[0]), (d_up, w[1])):
                part = jnp.dot(d, ref[:, at], preferred_element_type=F32)
                total = part if total is None else total + part
        out[:, at] = total.astype(BF)


def merge_kernel(in_ref, out_ref):
    rows = in_ref.shape[0] // 4
    width = out_ref.shape[1]
    data = []
    for local in range(2):
        both = [in_ref[y * rows : (y + 1) * rows, :].astype(F32) for y in (2 * local, 2 * local + 1)]
        total = (both[0] + both[1]).astype(BF)
        data += [total[:, :width], total[:, width:]]
    r = _iota((out_ref.shape[0], 4 * rows), 0)
    q = _iota((out_ref.shape[0], 4 * rows), 1)
    want = ((r // 2) % 2) * 2 * rows + ((r // 4) % 2) * rows + (r // 8) * 2 + r % 2
    out_ref[...] = jnp.dot(
        _select(q == want).astype(BF), jnp.concatenate(data, axis=0), preferred_element_type=F32
    ).astype(BF)


def final_kernel(in_ref, route_ref, out_ref):
    tok = out_ref.shape[0]
    rows, width = in_ref.shape
    r = _iota((rows, tok), 0)
    _, named, slot = _named(route_ref[...], 2 * (r // 8) + (r // 2) % 2)
    pick = named * _select(slot == (r % 2).astype(F32))
    data = in_ref[...]
    for h in range(2):
        mine = (pick * _select((r // 4) % 2 == h)).astype(BF)
        out_ref[:, h * width : (h + 1) * width] = lax.dot_general(
            mine, data, (((0,), (0,)), ((), ())), preferred_element_type=F32
        ).astype(BF)


def _shape(*dims):
    return jax.ShapeDtypeStruct(dims, BF)


def _call(kernel, out_shape, name, cost, vmem=16, **kw):
    return pl.pallas_call(
        kernel,
        out_shape=out_shape,
        name=name,
        cost_estimate=pl.CostEstimate(flops=cost[0], bytes_accessed=cost[1], transcendentals=0),
        compiler_params=pltpu.CompilerParams(vmem_limit_bytes=vmem * 1024 * 1024),
        **kw,
    )


def per_device(tokens, cotangent, gates, routes, w_gate, w_up, w_down):
    n_ex = lax.axis_size("ex")
    side = 4
    tok, width = tokens.shape
    unit = w_gate.shape[1]
    along_y = [[y * side + x for y in range(side)] for x in range(side)]

    def shift(v, d):
        return lax.ppermute(
            v, "hid", [(y * side + x, y * side + (x + d) % side) for y in range(side) for x in range(side)]
        )

    cut = (unit // 2 + 15) // 16 * 16
    early, late = _call(
        split_kernel,
        (_shape(3 * cut, width), _shape(3 * (unit - cut), width)),
        "split",
        (0, 12 * unit * width),
        in_specs=[pl.BlockSpec(memory_space=pltpu.HBM)] * 3,
        scratch_shapes=[pltpu.SemaphoreType.DMA((6,))],
    )(w_gate, w_up, w_down)
    def over_y(v):
        return lax.all_to_all(
            v, "hid", split_axis=0, concat_axis=0, tiled=True, axis_index_groups=along_y
        )

    small = (1 << 26, 1 << 21)
    packed = _call(pack_kernel, _shape(8 * n_ex, width), "pack", small, vmem=60,
        in_specs=[pl.BlockSpec(memory_space=pl.ANY)] * 4,
        scratch_shapes=[
            pltpu.VMEM(tokens.shape, BF),
            pltpu.VMEM(tokens.shape, BF),
            pltpu.VMEM(gates.shape[::-1], F32),
            pltpu.VMEM(routes.shape[::-1], jnp.int32),
            pltpu.SemaphoreType.DMA((4,)),
        ],
    )(tokens, cotangent, gates.T, routes.T)
    arrived = lax.all_to_all(packed, "ex", split_axis=0, concat_axis=0, tiled=True)
    left_early, right_late = shift(early, 1), shift(late, -1)
    left_late, right_early = shift(late, 1), shift(early, -1)
    own, other = _call(unpack_kernel, (_shape(4 * n_ex, width),) * 2, "unpack", small)(arrived)
    last = [shift(left_early, 1), shift(right_late, -1)]
    flip = lambda v, d: lax.ppermute(
        v, "hid", [(y * side + x, (y ^ d) * side + x) for y in range(side) for x in range(side)]
    )
    rows_all = [flip(other, 2), flip(other, 3), flip(own, 1), own]
    hid = side * unit
    main = 3 * unit // 256 * 256
    rest = 3 * unit - main
    staged = _call(
        stage_kernel,
        (_shape(main, width),) * 3 + (_shape(rest, width),) * 3,
        "stage",
        (0, 24 * 3 * unit * width),
        in_specs=[pl.BlockSpec(memory_space=pl.ANY)] * 7,
        scratch_shapes=[pltpu.SemaphoreType.DMA((18,))],
    )(w_gate, w_up, w_down, left_early, left_late, right_early, right_late)
    rows = 8 * n_ex
    parts = _call(
        grad_kernel,
        _shape(rows, width),
        "grad",
        (10 * rows * hid * width, 6 * hid * width),
        vmem=36,
        in_specs=[pl.BlockSpec(memory_space=pltpu.VMEM)] * 10 + [pl.BlockSpec(memory_space=pl.ANY)] * 2,
        scratch_shapes=[pltpu.VMEM((rows, width), BF)] * 2
        + [pltpu.VMEM((rest + unit, width), BF)] * 3
        + [pltpu.SemaphoreType.DMA((6,))],
    )(*rows_all, *staged, *last)
    merged = _call(merge_kernel, _shape(8 * n_ex, width // 2), "merge", small)(over_y(parts))
    landed = lax.all_to_all(merged, "ex", split_axis=0, concat_axis=0, tiled=True)
    return _call(final_kernel, _shape(tok, width), "final", small)(landed, routes.T)


def solution(mesh):
    split = P(("ex", "hid"), None)
    deep = P(("ex", "hid"), None, None)
    return jax.shard_map(
        per_device,
        mesh=mesh,
        in_specs=(split, split, split, split, deep, deep, deep),
        out_specs=split,
        check_vma=False,
    )
```

```python
import functools

import jax
import jax.numpy as jnp
from jax import lax
from jax.experimental import pallas as pl
from jax.experimental.pallas import tpu as pltpu
from jax.sharding import PartitionSpec as P

BF = jnp.bfloat16
F32 = jnp.float32
COLS = 4


def _iota(shape, axis):
    return lax.broadcasted_iota(jnp.int32, shape, axis)


def _select(cond):
    return jnp.where(cond, 1.0, 0.0).astype(F32)


def _named(routes, expert):
    top, tok = routes.shape
    each = [_select(routes[k : k + 1, :] == expert) for k in range(top)]
    named = functools.reduce(lambda a, b: a + b, each)
    earlier = _select(_iota((tok, tok), 0) < _iota((tok, tok), 1)).astype(BF)
    slot = jnp.dot(named.astype(BF), earlier, preferred_element_type=F32)
    return each, named, slot


def pack_kernel(tok_in, cot_in, gate_in, route_in, out_ref, tok_ref, cot_ref, gate_ref, route_ref, sem):
    copies = [
        pltpu.make_async_copy(src, dst, sem.at[i])
        for i, (src, dst) in enumerate(
            ((route_in, route_ref), (gate_in, gate_ref), (tok_in, tok_ref), (cot_in, cot_ref))
        )
    ]
    for cp in copies:
        cp.start()
    for cp in copies[:2]:
        cp.wait()
    tok, width = tok_ref.shape
    top = route_ref.shape[0]
    rows = out_ref.shape[0]
    r = _iota((rows, tok), 0)
    each, named, slot = _named(route_ref[...], r // 4)
    hit = _select(slot == (r % 2).astype(F32))
    is_x = _select((r // 2) % 2 == 0)
    weight = sum(each[k] * gate_ref[k : k + 1, :] for k in range(top))
    weight = jnp.sum(weight * hit * (1.0 - is_x) + is_x * (1.0 / tok), axis=1, keepdims=True)
    pick = named * hit
    pick = jnp.concatenate([pick * is_x, pick * (1.0 - is_x)], axis=1).astype(BF)
    for cp in copies[2:]:
        cp.wait()
    data = jnp.concatenate([tok_ref[...], cot_ref[...]], axis=0)
    out_ref[...] = (weight * jnp.dot(pick, data, preferred_element_type=F32)).astype(BF)


def split_kernel(*refs):
    w_in, outs, sem = refs[:3], refs[3:5], refs[5]
    cut = outs[0].shape[0] // 3
    copies = []
    for m, w in enumerate(w_in):
        for i, (at, size) in enumerate(((0, cut), (cut, w.shape[1] - cut))):
            copies.append(
                pltpu.make_async_copy(
                    w.at[0, pl.ds(at, size)], outs[i].at[pl.ds(m * size, size)], sem.at[2 * m + i]
                )
            )
    for cp in copies:
        cp.start()
    for cp in copies:
        cp.wait()


def unpack_kernel(in_ref, own_ref, other_ref):
    g = lax.axis_index("hid") // 8
    rows = own_ref.shape[0]
    half = rows // 2
    q = _iota((rows, in_ref.shape[0]), 0)
    r = _iota((rows, in_ref.shape[0]), 1)
    want = ((q % half) // 2) * 8 + (q // half) * 2 + q % 2
    data = in_ref[...]
    for o, ref in enumerate((own_ref, other_ref)):
        pick = _select(r == want + 4 * jnp.bitwise_xor(g, o)).astype(BF)
        ref[...] = jnp.dot(pick, data, preferred_element_type=F32).astype(BF)


def _parts(unit, first):
    return [(0, unit)] + [
        (unit * (1 + i // 2) + first * (i % 2), first if i % 2 == 0 else unit - first) for i in range(6)
    ]


def stage_kernel(*refs):
    own, moved, mains, rests, sem = refs[:3], refs[3:7], refs[7:10], refs[10:13], refs[13]
    unit, first = own[0].shape[1], moved[0].shape[0] // 3
    main = mains[0].shape[0]
    copies = []
    for m in range(3):
        for i, (at, size) in enumerate(_parts(unit, first)[:5]):
            src = own[m].at[0] if i == 0 else moved[i - 1].at[pl.ds(m * size, size)]
            fit = min(size, main - at)
            copies.append((src.at[pl.ds(0, fit)], mains[m].at[pl.ds(at, fit)]))
            if fit < size:
                copies.append((src.at[pl.ds(fit, size - fit)], rests[m]))
    copies = [pltpu.make_async_copy(src, dst, sem.at[i]) for i, (src, dst) in enumerate(copies)]
    for cp in copies:
        cp.start()
    for cp in copies:
        cp.wait()


def tail_kernel(*refs):
    rests, last, tails, sem = refs[:3], refs[3:5], refs[5:8], refs[8]
    copies = []
    for m in range(3):
        at = rests[m].shape[0]
        copies.append((rests[m], tails[m].at[pl.ds(0, at)]))
        for piece in last:
            size = piece.shape[0] // 3
            copies.append((piece.at[pl.ds(m * size, size)], tails[m].at[pl.ds(at, size)]))
            at += size
    copies = [pltpu.make_async_copy(src, dst, sem.at[i]) for i, (src, dst) in enumerate(copies)]
    for cp in copies:
        cp.start()
    for cp in copies:
        cp.wait()


def grad_kernel(*refs):
    n = 4
    rows_in, mains, tails, out = refs[:n], refs[n : n + 3], refs[n + 3 : n + 6], refs[n + 6]
    x, y = refs[n + 7 :]
    half = rows_in[0].shape[0] // 2
    me = lax.axis_index("hid") // n
    for i, d in enumerate((2, 3, 1, 0)):
        at = pl.ds(pl.multiple_of(jnp.bitwise_xor(me, d) * half, half), half)
        x[at, :] = rows_in[i][0:half, :]
        y[at, :] = rows_in[i][half : 2 * half, :]
    dims = (((1,), (1,)), ((), ()))
    dot = lambda a, w: lax.dot_general(a[...], w[...], dims, preferred_element_type=F32)
    inner = []
    for w in (mains, tails):
        gv, uv, hv = dot(x, w[0]), dot(x, w[1]), dot(y, w[2])
        sig = jax.nn.sigmoid(gv)
        d_up = (hv * gv * sig).astype(BF)
        d_gate = (hv * uv * sig * (1.0 + gv * (1.0 - sig))).astype(BF)
        inner.append((d_gate, d_up))
    width = out.shape[1]
    step = width // COLS
    for c in range(COLS):
        at = slice(c * step, (c + 1) * step)
        total = None
        for (d_gate, d_up), w in zip(inner, (mains, tails)):
            for d, ref in ((d_gate, w[0]), (d_up, w[1])):
                part = jnp.dot(d, ref[:, at], preferred_element_type=F32)
                total = part if total is None else total + part
        out[:, at] = total.astype(BF)


def merge_kernel(in_ref, out_ref):
    rows = in_ref.shape[0] // 4
    width = out_ref.shape[1]
    data = []
    for local in range(2):
        both = [in_ref[y * rows : (y + 1) * rows, :].astype(F32) for y in (2 * local, 2 * local + 1)]
        total = (both[0] + both[1]).astype(BF)
        data += [total[:, :width], total[:, width:]]
    r = _iota((out_ref.shape[0], 4 * rows), 0)
    q = _iota((out_ref.shape[0], 4 * rows), 1)
    want = ((r // 2) % 2) * 2 * rows + ((r // 4) % 2) * rows + (r // 8) * 2 + r % 2
    out_ref[...] = jnp.dot(
        _select(q == want).astype(BF), jnp.concatenate(data, axis=0), preferred_element_type=F32
    ).astype(BF)


def final_kernel(in_ref, route_ref, out_ref):
    tok = out_ref.shape[0]
    rows, width = in_ref.shape
    r = _iota((rows, tok), 0)
    _, named, slot = _named(route_ref[...], 2 * (r // 8) + (r // 2) % 2)
    pick = named * _select(slot == (r % 2).astype(F32))
    data = in_ref[...]
    for h in range(2):
        mine = (pick * _select((r // 4) % 2 == h)).astype(BF)
        out_ref[:, h * width : (h + 1) * width] = lax.dot_general(
            mine, data, (((0,), (0,)), ((), ())), preferred_element_type=F32
        ).astype(BF)


def _shape(*dims):
    return jax.ShapeDtypeStruct(dims, BF)


def _call(kernel, out_shape, name, cost, vmem=16, **kw):
    return pl.pallas_call(
        kernel,
        out_shape=out_shape,
        name=name,
        cost_estimate=pl.CostEstimate(flops=cost[0], bytes_accessed=cost[1], transcendentals=0),
        compiler_params=pltpu.CompilerParams(vmem_limit_bytes=vmem * 1024 * 1024),
        **kw,
    )


def per_device(tokens, cotangent, gates, routes, w_gate, w_up, w_down):
    n_ex = lax.axis_size("ex")
    side = 4
    tok, width = tokens.shape
    unit = w_gate.shape[1]
    along_y = [[y * side + x for y in range(side)] for x in range(side)]

    def shift(v, d):
        return lax.ppermute(
            v, "hid", [(y * side + x, y * side + (x + d) % side) for y in range(side) for x in range(side)]
        )

    cut = (unit // 2 + 15) // 16 * 16
    early, late = _call(
        split_kernel,
        (_shape(3 * cut, width), _shape(3 * (unit - cut), width)),
        "split",
        (0, 12 * unit * width),
        in_specs=[pl.BlockSpec(memory_space=pltpu.HBM)] * 3,
        scratch_shapes=[pltpu.SemaphoreType.DMA((6,))],
    )(w_gate, w_up, w_down)
    def over_y(v):
        return lax.all_to_all(
            v, "hid", split_axis=0, concat_axis=0, tiled=True, axis_index_groups=along_y
        )

    small = (1 << 26, 1 << 21)
    packed = _call(pack_kernel, _shape(8 * n_ex, width), "pack", small, vmem=60,
        in_specs=[pl.BlockSpec(memory_space=pl.ANY)] * 4,
        scratch_shapes=[
            pltpu.VMEM(tokens.shape, BF),
            pltpu.VMEM(tokens.shape, BF),
            pltpu.VMEM(gates.shape[::-1], F32),
            pltpu.VMEM(routes.shape[::-1], jnp.int32),
            pltpu.SemaphoreType.DMA((4,)),
        ],
    )(tokens, cotangent, gates.T, routes.T)
    arrived = lax.all_to_all(packed, "ex", split_axis=0, concat_axis=0, tiled=True)
    left_early, right_late = shift(early, 1), shift(late, -1)
    left_late, right_early = shift(late, 1), shift(early, -1)
    own, other = _call(unpack_kernel, (_shape(4 * n_ex, width),) * 2, "unpack", small)(arrived)
    last = [shift(left_early, 1), shift(right_late, -1)]
    flip = lambda v, d: lax.ppermute(
        v, "hid", [(y * side + x, (y ^ d) * side + x) for y in range(side) for x in range(side)]
    )
    rows_all = [flip(other, 2), flip(other, 3), flip(own, 1), own]
    hid = side * unit
    main = 3 * unit // 256 * 256
    rest = 3 * unit - main
    staged = _call(
        stage_kernel,
        (_shape(main, width),) * 3 + (_shape(rest, width),) * 3,
        "stage",
        (0, 24 * 3 * unit * width),
        in_specs=[pl.BlockSpec(memory_space=pl.ANY)] * 7,
        scratch_shapes=[pltpu.SemaphoreType.DMA((18,))],
    )(w_gate, w_up, w_down, left_early, left_late, right_early, right_late)
    tails = _call(
        tail_kernel,
        (_shape(rest + unit, width),) * 3,
        "tail",
        (0, 12 * (rest + unit) * width),
        in_specs=[pl.BlockSpec(memory_space=pl.ANY)] * 5,
        scratch_shapes=[pltpu.SemaphoreType.DMA((9,))],
    )(*staged[3:], *last)
    rows = 8 * n_ex
    parts = _call(
        grad_kernel,
        _shape(rows, width),
        "grad",
        (10 * rows * hid * width, 6 * hid * width),
        vmem=36,
        scratch_shapes=[pltpu.VMEM((rows, width), BF)] * 2,
    )(*rows_all, *staged[:3], *tails)
    merged = _call(merge_kernel, _shape(8 * n_ex, width // 2), "merge", small)(over_y(parts))
    landed = lax.all_to_all(merged, "ex", split_axis=0, concat_axis=0, tiled=True)
    return _call(final_kernel, _shape(tok, width), "final", small)(landed, routes.T)


def solution(mesh):
    split = P(("ex", "hid"), None)
    deep = P(("ex", "hid"), None, None)
    return jax.shard_map(
        per_device,
        mesh=mesh,
        in_specs=(split, split, split, split, deep, deep, deep),
        out_specs=split,
        check_vma=False,
    )
```

```python
import functools

import jax
import jax.numpy as jnp
from jax import lax
from jax.experimental import pallas as pl
from jax.experimental.pallas import tpu as pltpu
from jax.sharding import PartitionSpec as P

BF = jnp.bfloat16
F32 = jnp.float32
COLS = 4


def _iota(shape, axis):
    return lax.broadcasted_iota(jnp.int32, shape, axis)


def _select(cond):
    return jnp.where(cond, 1.0, 0.0).astype(F32)


def _named(routes, expert):
    top, tok = routes.shape
    each = [_select(routes[k : k + 1, :] == expert) for k in range(top)]
    named = functools.reduce(lambda a, b: a + b, each)
    earlier = _select(_iota((tok, tok), 0) < _iota((tok, tok), 1)).astype(BF)
    slot = jnp.dot(named.astype(BF), earlier, preferred_element_type=F32)
    return each, named, slot


def pack_kernel(tok_in, cot_in, gate_in, route_in, out_ref, tok_ref, cot_ref, gate_ref, route_ref, sem):
    copies = [
        pltpu.make_async_copy(src, dst, sem.at[i])
        for i, (src, dst) in enumerate(
            ((route_in, route_ref), (gate_in, gate_ref), (tok_in, tok_ref), (cot_in, cot_ref))
        )
    ]
    for cp in copies:
        cp.start()
    for cp in copies[:2]:
        cp.wait()
    tok, width = tok_ref.shape
    top = route_ref.shape[0]
    rows = out_ref.shape[0]
    r = _iota((rows, tok), 0)
    each, named, slot = _named(route_ref[...], r // 4)
    hit = _select(slot == (r % 2).astype(F32))
    is_x = _select((r // 2) % 2 == 0)
    weight = sum(each[k] * gate_ref[k : k + 1, :] for k in range(top))
    weight = jnp.sum(weight * hit * (1.0 - is_x) + is_x * (1.0 / tok), axis=1, keepdims=True)
    pick = named * hit
    pick = jnp.concatenate([pick * is_x, pick * (1.0 - is_x)], axis=1).astype(BF)
    for cp in copies[2:]:
        cp.wait()
    data = jnp.concatenate([tok_ref[...], cot_ref[...]], axis=0)
    out_ref[...] = (weight * jnp.dot(pick, data, preferred_element_type=F32)).astype(BF)


def split_kernel(at, g_in, u_in, d_in, out, sem):
    size = out.shape[0] // 3
    copies = [
        pltpu.make_async_copy(w.at[0, pl.ds(at, size)], out.at[pl.ds(m * size, size)], sem.at[m])
        for m, w in enumerate((g_in, u_in, d_in))
    ]
    for cp in copies:
        cp.start()
    for cp in copies:
        cp.wait()


def unpack_kernel(in_ref, own_ref, other_ref):
    g = lax.axis_index("hid") // 8
    rows = own_ref.shape[0]
    half = rows // 2
    q = _iota((rows, in_ref.shape[0]), 0)
    r = _iota((rows, in_ref.shape[0]), 1)
    want = ((q % half) // 2) * 8 + (q // half) * 2 + q % 2
    data = in_ref[...]
    for o, ref in enumerate((own_ref, other_ref)):
        pick = _select(r == want + 4 * jnp.bitwise_xor(g, o)).astype(BF)
        ref[...] = jnp.dot(pick, data, preferred_element_type=F32).astype(BF)


def _parts(unit, first):
    return [(0, unit)] + [
        (unit * (1 + i // 2) + first * (i % 2), first if i % 2 == 0 else unit - first) for i in range(6)
    ]


def stage_kernel(*refs):
    own, moved, mains, rests, sem = refs[:3], refs[3:7], refs[7:10], refs[10:13], refs[13]
    unit, first = own[0].shape[1], moved[0].shape[0] // 3
    main = mains[0].shape[0]
    copies = []
    for m in range(3):
        for i, (at, size) in enumerate(_parts(unit, first)[:5]):
            src = own[m].at[0] if i == 0 else moved[i - 1].at[pl.ds(m * size, size)]
            fit = min(size, main - at)
            copies.append((src.at[pl.ds(0, fit)], mains[m].at[pl.ds(at, fit)]))
            if fit < size:
                copies.append((src.at[pl.ds(fit, size - fit)], rests[m]))
    copies = [pltpu.make_async_copy(src, dst, sem.at[i]) for i, (src, dst) in enumerate(copies)]
    for cp in copies:
        cp.start()
    for cp in copies:
        cp.wait()


def tail_kernel(*refs):
    rests, last, tails, sem = refs[:3], refs[3:5], refs[5:8], refs[8]
    copies = []
    for m in range(3):
        at = rests[m].shape[0]
        copies.append((rests[m], tails[m].at[pl.ds(0, at)]))
        for piece in last:
            size = piece.shape[0] // 3
            copies.append((piece.at[pl.ds(m * size, size)], tails[m].at[pl.ds(at, size)]))
            at += size
    copies = [pltpu.make_async_copy(src, dst, sem.at[i]) for i, (src, dst) in enumerate(copies)]
    for cp in copies:
        cp.start()
    for cp in copies:
        cp.wait()


def grad_kernel(*refs):
    n = 4
    rows_in, mains, tails, out = refs[:n], refs[n : n + 3], refs[n + 3 : n + 6], refs[n + 6]
    x, y = refs[n + 7 :]
    half = rows_in[0].shape[0] // 2
    me = lax.axis_index("hid") // n
    for i, d in enumerate((2, 3, 1, 0)):
        at = pl.ds(pl.multiple_of(jnp.bitwise_xor(me, d) * half, half), half)
        x[at, :] = rows_in[i][0:half, :]
        y[at, :] = rows_in[i][half : 2 * half, :]
    dims = (((1,), (1,)), ((), ()))
    dot = lambda a, w: lax.dot_general(a[...], w[...], dims, preferred_element_type=F32)
    inner = []
    for w in (mains, tails):
        gv, uv, hv = dot(x, w[0]), dot(x, w[1]), dot(y, w[2])
        sig = jax.nn.sigmoid(gv)
        d_up = (hv * gv * sig).astype(BF)
        d_gate = (hv * uv * sig * (1.0 + gv * (1.0 - sig))).astype(BF)
        inner.append((d_gate, d_up))
    width = out.shape[1]
    step = width // COLS
    for c in range(COLS):
        at = slice(c * step, (c + 1) * step)
        total = None
        for (d_gate, d_up), w in zip(inner, (mains, tails)):
            for d, ref in ((d_gate, w[0]), (d_up, w[1])):
                part = jnp.dot(d, ref[:, at], preferred_element_type=F32)
                total = part if total is None else total + part
        out[:, at] = total.astype(BF)


def merge_kernel(in_ref, out_ref):
    rows = in_ref.shape[0] // 4
    width = out_ref.shape[1]
    data = []
    for local in range(2):
        both = [in_ref[y * rows : (y + 1) * rows, :].astype(F32) for y in (2 * local, 2 * local + 1)]
        total = (both[0] + both[1]).astype(BF)
        data += [total[:, :width], total[:, width:]]
    r = _iota((out_ref.shape[0], 4 * rows), 0)
    q = _iota((out_ref.shape[0], 4 * rows), 1)
    want = ((r // 2) % 2) * 2 * rows + ((r // 4) % 2) * rows + (r // 8) * 2 + r % 2
    out_ref[...] = jnp.dot(
        _select(q == want).astype(BF), jnp.concatenate(data, axis=0), preferred_element_type=F32
    ).astype(BF)


def final_kernel(in_ref, route_ref, out_ref):
    tok = out_ref.shape[0]
    rows, width = in_ref.shape
    r = _iota((rows, tok), 0)
    _, named, slot = _named(route_ref[...], 2 * (r // 8) + (r // 2) % 2)
    pick = named * _select(slot == (r % 2).astype(F32))
    data = in_ref[...]
    for h in range(2):
        mine = (pick * _select((r // 4) % 2 == h)).astype(BF)
        out_ref[:, h * width : (h + 1) * width] = lax.dot_general(
            mine, data, (((0,), (0,)), ((), ())), preferred_element_type=F32
        ).astype(BF)


def _shape(*dims):
    return jax.ShapeDtypeStruct(dims, BF)


def _call(kernel, out_shape, name, cost, vmem=16, **kw):
    return pl.pallas_call(
        kernel,
        out_shape=out_shape,
        name=name,
        cost_estimate=pl.CostEstimate(flops=cost[0], bytes_accessed=cost[1], transcendentals=0),
        compiler_params=pltpu.CompilerParams(vmem_limit_bytes=vmem * 1024 * 1024),
        **kw,
    )


def per_device(tokens, cotangent, gates, routes, w_gate, w_up, w_down):
    n_ex = lax.axis_size("ex")
    side = 4
    tok, width = tokens.shape
    unit = w_gate.shape[1]
    along_y = [[y * side + x for y in range(side)] for x in range(side)]

    def shift(v, d):
        return lax.ppermute(
            v, "hid", [(y * side + x, y * side + (x + d) % side) for y in range(side) for x in range(side)]
        )

    cut = (unit // 2 + 15) // 16 * 16
    early, late = [
        _call(
            functools.partial(split_kernel, at),
            _shape(3 * size, width),
            name,
            (0, 12 * size * width),
            in_specs=[pl.BlockSpec(memory_space=pltpu.HBM)] * 3,
            out_specs=pl.BlockSpec(memory_space=pl.ANY),
            scratch_shapes=[pltpu.SemaphoreType.DMA((3,))],
        )(w_gate, w_up, w_down)
        for name, at, size in (("early", 0, cut), ("late", cut, unit - cut))
    ]

    def over_y(v):
        return lax.all_to_all(
            v, "hid", split_axis=0, concat_axis=0, tiled=True, axis_index_groups=along_y
        )

    small = (1 << 26, 1 << 21)
    packed = _call(pack_kernel, _shape(8 * n_ex, width), "pack", small, vmem=60,
        in_specs=[pl.BlockSpec(memory_space=pl.ANY)] * 4,
        scratch_shapes=[
            pltpu.VMEM(tokens.shape, BF),
            pltpu.VMEM(tokens.shape, BF),
            pltpu.VMEM(gates.shape[::-1], F32),
            pltpu.VMEM(routes.shape[::-1], jnp.int32),
            pltpu.SemaphoreType.DMA((4,)),
        ],
    )(tokens, cotangent, gates.T, routes.T)
    arrived = lax.all_to_all(packed, "ex", split_axis=0, concat_axis=0, tiled=True)
    left_early, right_late = shift(early, 1), shift(late, -1)
    left_late, right_early = shift(late, 1), shift(early, -1)
    own, other = _call(unpack_kernel, (_shape(4 * n_ex, width),) * 2, "unpack", small)(arrived)
    last = [shift(left_early, 1), shift(right_late, -1)]
    flip = lambda v, d: lax.ppermute(
        v, "hid", [(y * side + x, (y ^ d) * side + x) for y in range(side) for x in range(side)]
    )
    rows_all = [flip(other, 2), flip(other, 3), flip(own, 1), own]
    hid = side * unit
    main = 3 * unit // 256 * 256
    rest = 3 * unit - main
    staged = _call(
        stage_kernel,
        (_shape(main, width),) * 3 + (_shape(rest, width),) * 3,
        "stage",
        (0, 24 * 3 * unit * width),
        in_specs=[pl.BlockSpec(memory_space=pl.ANY)] * 7,
        scratch_shapes=[pltpu.SemaphoreType.DMA((18,))],
    )(w_gate, w_up, w_down, left_early, left_late, right_early, right_late)
    tails = _call(
        tail_kernel,
        (_shape(rest + unit, width),) * 3,
        "tail",
        (0, 12 * (rest + unit) * width),
        in_specs=[pl.BlockSpec(memory_space=pl.ANY)] * 5,
        scratch_shapes=[pltpu.SemaphoreType.DMA((9,))],
    )(*staged[3:], *last)
    rows = 8 * n_ex
    parts = _call(
        grad_kernel,
        _shape(rows, width),
        "grad",
        (10 * rows * hid * width, 6 * hid * width),
        vmem=36,
        scratch_shapes=[pltpu.VMEM((rows, width), BF)] * 2,
    )(*rows_all, *staged[:3], *tails)
    merged = _call(merge_kernel, _shape(8 * n_ex, width // 2), "merge", small)(over_y(parts))
    landed = lax.all_to_all(merged, "ex", split_axis=0, concat_axis=0, tiled=True)
    return _call(final_kernel, _shape(tok, width), "final", small)(landed, routes.T)


def solution(mesh):
    split = P(("ex", "hid"), None)
    deep = P(("ex", "hid"), None, None)
    return jax.shard_map(
        per_device,
        mesh=mesh,
        in_specs=(split, split, split, split, deep, deep, deep),
        out_specs=split,
        check_vma=False,
    )
```
